32 devices in a mesh: ctx: 16 (over z, y, core), fsdp: 2 (over x).
Axes of the slice: x: 2, y: 2, z: 4, core: 2. Of those that a mesh axis runs over, the one named last changes fastest.
Arguments:
- tokens: bfloat16 [2048, 4096], P('ctx', 'fsdp'), may hold values from -130 to 130, as said below
- w_query: bfloat16 [4096, 4096], P('ctx', 'fsdp'), may hold values from -0.09375 to 0.09375
- key_matrix: bfloat16 [4096, 1024], P('ctx', 'fsdp'), may hold values from -0.09375 to 0.09375
- value_matrix: bfloat16 [4096, 1024], P('ctx', 'fsdp'), may hold values from -0.09375 to 0.09375
- w_out: bfloat16 [4096, 4096], P('fsdp', 'ctx'), may hold values from -0.75 to 0.75
Outputs:
- mixed: bfloat16 [2048, 4096], P('ctx', 'fsdp')
The draws below stay inside these ranges and needn't reach their ends.
Inputs may be any that keep to these rules, and one draw needn't show every extreme that they name: `tokens`: no structure of the entries is promised.
All inputs are finite; a program needn't handle non-finite values.
Results may differ from the reference program's by a relative error of at most 0.014.
The reference program's roundings to bfloat16 on the way count: a program that leaves them out, or rounds other values in their place, can miss the bound.
Values may be sent and summed in bfloat16 or wider, within the bound.
No kernel may reach another device: no remote copies, remote signals or barrier semaphores. Data moves between devices by JAX's collectives and lax.ppermute only.
A program may use at most 128 MiB of HBM per device.

```python
import math
import jax
import jax.numpy as jnp
from jax import lax

MODEL_WIDTH = 4096
QUERY_HEADS = 32
SHARED_HEADS = 8
HEAD_SIZE = 128
EVENT_WINDOW = 2048
N_FSDP = 2


def draw_tokens(key, part):
    noise_key = jax.random.fold_in(key, 11)
    gauss_rows = jax.random.truncated_normal(noise_key, -6.0, 6.0, (EVENT_WINDOW, MODEL_WIDTH), jnp.float32) * 1.5
    return gauss_rows.astype(jnp.bfloat16)


def levels(stream_key, extent, shards, smallest, largest):
    def one(axis_at, parts):
        draws = jax.random.uniform(jax.random.fold_in(jax.random.fold_in(stream_key, 6), axis_at), (parts,), jnp.float32, smallest / len(shards), largest / len(shards))
        return jnp.repeat(jnp.exp(draws), extent[axis_at] // parts).reshape((-1,) + (1,) * (len(extent) - axis_at - 1))

    factor_of = one(*shards[0])
    for cut in shards[1:]:
        factor_of = factor_of * one(*cut)
    return factor_of


def noise(key, extent, scale, reach, shards=(), kind=jnp.bfloat16):
    array = jax.random.normal(key, extent, jnp.float32) * scale
    if len(shards) > 0:
        array = levels(key, extent, shards, -0.22, 0.18) * array
    return jnp.clip(array, min=-reach, max=reach).astype(kind)


def setup_inputs(seed: int = 0) -> dict:
    streams_of = jax.random.split(jax.random.key(seed), 6)
    return {
        "tokens": draw_tokens(jax.random.fold_in(streams_of[5], 71), 0),
        "w_query": noise(streams_of[1], (MODEL_WIDTH, QUERY_HEADS * HEAD_SIZE), MODEL_WIDTH ** -0.5, 0.09375, ((0, 16), (1, 2))),
        "key_matrix": noise(streams_of[2], (MODEL_WIDTH, SHARED_HEADS * HEAD_SIZE), MODEL_WIDTH ** -0.5, 0.09375, ((0, 16), (1, 2))),
        "value_matrix": noise(streams_of[3], (MODEL_WIDTH, SHARED_HEADS * HEAD_SIZE), MODEL_WIDTH ** -0.5, 0.09375, ((0, 16), (1, 2))),
        "w_out": noise(streams_of[4], (QUERY_HEADS * HEAD_SIZE, MODEL_WIDTH), 64 ** -0.5, 0.75, ((0, 2), (1, 16))),
    }


def rotate_heads(values, positions):
    tok_count = values.shape[0]
    head_count = values.shape[1] // HEAD_SIZE
    half_dim = HEAD_SIZE // 2
    inverse_freq = jnp.power(jnp.float32(500000.0), -jnp.arange(half_dim, dtype=jnp.float32) * 2.0 / HEAD_SIZE)
    angles = positions.astype(jnp.float32)[:, None] * inverse_freq[None, :]
    cosine = jnp.cos(angles)[:, None, :]
    sine_table = jnp.sin(angles)[:, None, :]
    shaped = values.reshape(tok_count, head_count, HEAD_SIZE)
    first_half = shaped[:, :, :half_dim]
    second = shaped[:, :, half_dim:]
    turned = jnp.concatenate([first_half * cosine - second * sine_table, second * cosine + first_half * sine_table], axis=2)
    return turned.reshape(tok_count, head_count * HEAD_SIZE).astype(jnp.bfloat16)

def reference(tokens, w_query, key_matrix, value_matrix, w_out):
    positions = jnp.arange(EVENT_WINDOW, dtype=jnp.int32)
    queries = rotate_heads(jnp.dot(tokens, w_query, preferred_element_type=jnp.float32), positions)
    projected_keys = rotate_heads(jnp.dot(tokens, key_matrix, preferred_element_type=jnp.float32), positions)
    projected_values = jnp.dot(tokens, value_matrix, preferred_element_type=jnp.float32).astype(jnp.bfloat16)
    queries_per_group = QUERY_HEADS // SHARED_HEADS
    expanded_keys = jnp.repeat(projected_keys.reshape(EVENT_WINDOW, SHARED_HEADS, HEAD_SIZE).astype(jnp.float32), queries_per_group, axis=1)
    expanded_values = jnp.repeat(projected_values.reshape(EVENT_WINDOW, SHARED_HEADS, HEAD_SIZE).astype(jnp.float32), queries_per_group, axis=1)
    block_rows = min(512, EVENT_WINDOW)
    score_scale = 1.0 / math.sqrt(HEAD_SIZE)

    def attend(block_index):
        begin = (block_index * block_rows).astype(jnp.int32)
        query_block = lax.dynamic_slice_in_dim(queries, begin, block_rows, 0).reshape(block_rows, QUERY_HEADS, HEAD_SIZE).astype(jnp.float32)
        scores = jnp.einsum('qhd,khd->hqk', query_block, expanded_keys) * score_scale
        query_pos = begin + jnp.arange(block_rows, dtype=jnp.int32)
        allowed = positions[None, None, :] <= query_pos[None, :, None]
        masked = jnp.where(allowed, scores, jnp.float32(-1e+30))
        row_max = lax.optimization_barrier(jnp.max(masked, axis=2, keepdims=True))
        exp_weights = jnp.where(allowed, jnp.exp(masked - row_max), jnp.float32(0.0))
        row_total = lax.optimization_barrier(jnp.sum(exp_weights, axis=2))
        rounded = exp_weights.astype(jnp.bfloat16).astype(jnp.float32)
        summed = jnp.einsum('hqk,khd->hqd', rounded, expanded_values)
        normed = summed / row_total[:, :, None]
        return normed.transpose(1, 0, 2).reshape(block_rows, QUERY_HEADS * HEAD_SIZE).astype(jnp.bfloat16)
    attn_out = lax.map(attend, jnp.arange(EVENT_WINDOW // block_rows, dtype=jnp.int32)).reshape(EVENT_WINDOW, QUERY_HEADS * HEAD_SIZE)
    group_width = QUERY_HEADS * HEAD_SIZE // N_FSDP
    total_out = jnp.zeros((EVENT_WINDOW, MODEL_WIDTH), jnp.float32)
    for group_index in range(N_FSDP):
        low = group_index * group_width
        group_term = jnp.dot(attn_out[:, low:low + group_width], w_out[low:low + group_width], preferred_element_type=jnp.float32)
        rounded_term = lax.optimization_barrier(group_term.astype(jnp.bfloat16))
        total_out = total_out + rounded_term.astype(jnp.float32)
    return total_out.astype(jnp.bfloat16)
```

```python
import functools
import math

import jax
import jax.numpy as jnp
from jax import lax
from jax.experimental import pallas as pl
from jax.experimental.pallas import tpu as pltpu
from jax.sharding import PartitionSpec as P

HEAD_SIZE = 128
AXES = ("ctx", "fsdp")
VMEM_LIMIT = 48 * 1024 * 1024


def rotary_tables(positions):
    half_dim = HEAD_SIZE // 2
    inverse_freq = jnp.power(
        jnp.float32(500000.0), -jnp.arange(half_dim, dtype=jnp.float32) * 2.0 / HEAD_SIZE
    )
    angles = positions.astype(jnp.float32)[:, None] * inverse_freq[None, :]
    return jnp.cos(angles), jnp.sin(angles)


def rotate_heads(values, positions):
    tok_count = values.shape[0]
    head_count = values.shape[1] // HEAD_SIZE
    half_dim = HEAD_SIZE // 2
    cosine, sine_table = rotary_tables(positions)
    cosine, sine_table = cosine[:, None, :], sine_table[:, None, :]
    shaped = values.reshape(tok_count, head_count, HEAD_SIZE)
    first_half = shaped[:, :, :half_dim]
    second = shaped[:, :, half_dim:]
    turned = jnp.concatenate(
        [first_half * cosine - second * sine_table, second * cosine + first_half * sine_table],
        axis=2,
    )
    return turned.reshape(tok_count, head_count * HEAD_SIZE).astype(jnp.bfloat16)


def gathered_body(tokens, w_query, key_matrix, value_matrix, w_out):
    features = lax.all_gather(tokens, "fsdp", axis=1, tiled=True)
    tok_count = features.shape[0]
    positions = lax.axis_index("ctx") * tok_count + jnp.arange(tok_count, dtype=jnp.int32)

    def add_rows(weight_piece):
        return jnp.dot(features, weight_piece, preferred_element_type=jnp.float32)

    query_sum = add_rows(lax.all_gather(w_query, "ctx", axis=0, tiled=True))
    key_sum = add_rows(lax.all_gather(key_matrix, "ctx", axis=0, tiled=True))
    value_sum = add_rows(lax.all_gather(value_matrix, "ctx", axis=0, tiled=True))
    queries = rotate_heads(query_sum, positions)
    projected_keys = rotate_heads(key_sum, positions)
    projected_values = value_sum.astype(jnp.bfloat16)
    kv_heads = projected_keys.shape[1] // HEAD_SIZE
    queries_per_group = queries.shape[1] // projected_keys.shape[1]
    stacked = (
        queries.reshape(tok_count, kv_heads, queries_per_group, HEAD_SIZE)
        .transpose(1, 2, 0, 3)
        .reshape(kv_heads, queries_per_group * tok_count, HEAD_SIZE)
    )
    query_pos = jnp.tile(positions, queries_per_group)
    score_scale = 1.0 / math.sqrt(HEAD_SIZE)

    def update(attn_state, key_block, value_block, key_start):
        row_max, row_total, accum = attn_state
        block_rows = key_block.shape[0]
        key_heads = key_block.reshape(block_rows, kv_heads, HEAD_SIZE)
        value_heads = value_block.reshape(block_rows, kv_heads, HEAD_SIZE)
        scores = (
            jnp.einsum("gqd,kgd->gqk", stacked, key_heads, preferred_element_type=jnp.float32)
            * score_scale
        )
        key_pos = key_start + jnp.arange(block_rows, dtype=jnp.int32)
        allowed = (key_pos[None, :] <= query_pos[:, None])[None]
        masked = jnp.where(allowed, scores, jnp.float32(-1e30))
        new_max = jnp.maximum(row_max, jnp.max(masked, axis=2))
        exp_weights = jnp.where(allowed, jnp.exp(masked - new_max[:, :, None]), jnp.float32(0.0))
        factor = jnp.exp(row_max - new_max)
        row_total = row_total * factor + jnp.sum(exp_weights, axis=2)
        accum = accum * factor[:, :, None] + jnp.einsum(
            "gqk,kgd->gqd",
            exp_weights.astype(jnp.bfloat16),
            value_heads,
            preferred_element_type=jnp.float32,
        )
        return (new_max, row_total, accum)

    query_rows = queries_per_group * tok_count
    initial = (
        jnp.full((kv_heads, query_rows), -1e30, jnp.float32),
        jnp.zeros((kv_heads, query_rows), jnp.float32),
        jnp.zeros((kv_heads, query_rows, HEAD_SIZE), jnp.float32),
    )
    key_piece = lax.all_gather(projected_keys, "ctx", axis=0, tiled=True)
    value_piece = lax.all_gather(projected_values, "ctx", axis=0, tiled=True)
    block_rows = min(tok_count, key_piece.shape[0])
    block_count = key_piece.shape[0] // block_rows

    def advance(block_index, carried):
        key_start = block_index * block_rows
        key_block = lax.dynamic_slice_in_dim(key_piece, block_index * block_rows, block_rows, 0)
        value_block = lax.dynamic_slice_in_dim(value_piece, block_index * block_rows, block_rows, 0)
        return update(carried, key_block, value_block, key_start)

    row_max, row_total, accum = lax.fori_loop(0, block_count, advance, initial)
    normed = accum / row_total[:, :, None]
    attn_out = (
        normed.reshape(kv_heads, queries_per_group, tok_count, HEAD_SIZE)
        .transpose(2, 0, 1, 3)
        .reshape(tok_count, kv_heads * queries_per_group * HEAD_SIZE)
        .astype(jnp.bfloat16)
    )
    partial_out = jnp.dot(
        attn_out,
        lax.all_gather(w_out, "ctx", axis=1, tiled=True),
        preferred_element_type=jnp.float32,
    )
    return lax.psum_scatter(
        partial_out.astype(jnp.bfloat16), "fsdp", scatter_dimension=1, tiled=True
    )


def moves(target):
    pairs = []
    for i in range(32):
        z, y, c, x = i // 8, i // 4 % 2, i // 2 % 2, i % 2
        tz, ty, tc, tx = target(z, y, c, x)
        pairs.append((i, tz * 8 + ty * 4 + tc * 2 + tx))
    return pairs


def move(array, target):
    return lax.ppermute(array, AXES, moves(target))


def across_z(array, m):
    return move(array, lambda z, y, c, x: (z ^ m, y, c, x))


def across_y(array):
    return move(array, lambda z, y, c, x: (z, 1 - y, c, x))


def across_core(array):
    return move(array, lambda z, y, c, x: (z, y, 1 - c, x))


def across_x(array):
    return move(array, lambda z, y, c, x: (z, y, c, 1 - x))


def any_specs(count):
    return [pl.BlockSpec(memory_space=pl.ANY)] * count


def smem_spec():
    return pl.BlockSpec(memory_space=pltpu.SMEM)


def vmem_spec():
    return pl.BlockSpec(memory_space=pltpu.VMEM)


def load_projection(place, token_refs, weight_refs, tok, wgt, sems):
    ctx, x = place[0], place[1]
    rows, half = token_refs[0].shape
    copies = []
    for m in range(4):
        for rx in range(2):
            into = tok.at[pl.ds(m * rows, rows), pl.ds(pl.multiple_of((x ^ rx) * half, half), half)]
            copies.append((token_refs[m * 2 + rx], into))
    for r, ref in enumerate(weight_refs):
        for m in range(4):
            block = ctx ^ (4 * m + r)
            depth = ref.shape[1]
            copies.append((ref.at[m], wgt.at[pl.ds(pl.multiple_of(block * depth, depth), depth)]))
    handles = [pltpu.make_async_copy(s, d, sems.at[i]) for i, (s, d) in enumerate(copies)]
    for handle in handles:
        handle.start()
    for handle in handles:
        handle.wait()


def rotated(values, cosine, sine):
    turned = jnp.concatenate([values[:, HEAD_SIZE // 2 :], values[:, : HEAD_SIZE // 2]], axis=1)
    return values * cosine + turned * sine


def kv_kernel(place, *refs):
    token_refs, weight_refs = refs[:8], refs[8:12]
    cosine, sine, out, tok, wgt, sems = refs[12:]
    load_projection(place, token_refs, weight_refs, tok, wgt, sems)
    rows = tok.shape[0] // 4
    values = jnp.dot(tok[...], wgt[...], preferred_element_type=jnp.float32)
    keys = rotated(values[:, :HEAD_SIZE], cosine[...], sine[...]).astype(jnp.bfloat16)
    vals = values[:, HEAD_SIZE:].astype(jnp.bfloat16)
    for m in range(4):
        out[m, :, :HEAD_SIZE] = keys[m * rows : (m + 1) * rows]
        out[m, :, HEAD_SIZE:] = vals[m * rows : (m + 1) * rows]


def query_kernel(place, *refs):
    token_refs, weight_refs = refs[:8], refs[8:12]
    cosine, sine, out, tok, wgt, sems = refs[12:]
    load_projection(place, token_refs, weight_refs, tok, wgt, sems)
    rows = tok.shape[0] // 4
    heads = wgt.shape[1] // HEAD_SIZE
    for pair in range(heads // 2):
        values = jnp.dot(
            tok[...],
            wgt[:, pair * 2 * HEAD_SIZE : (pair + 1) * 2 * HEAD_SIZE],
            preferred_element_type=jnp.float32,
        )
        for k in range(2):
            one = rotated(values[:, k * HEAD_SIZE : (k + 1) * HEAD_SIZE], cosine[...], sine[...])
            one = one.astype(jnp.bfloat16)
            head = pair * 2 + k
            for m in range(4):
                out[m, head * rows : (head + 1) * rows, :] = one[m * rows : (m + 1) * rows]


def project(kernel, out_shape, place, tokens, weights, cosine, sine):
    rows, half = tokens[0].shape
    _, depth, width = weights[0].shape
    flops = 2 * 4 * rows * 16 * depth * width
    return pl.pallas_call(
        kernel,
        out_shape=jax.ShapeDtypeStruct(out_shape, jnp.bfloat16),
        in_specs=[smem_spec()] + any_specs(12) + [vmem_spec()] * 2,
        out_specs=vmem_spec(),
        scratch_shapes=[
            pltpu.VMEM((4 * rows, 2 * half), jnp.bfloat16),
            pltpu.VMEM((16 * depth, width), jnp.bfloat16),
            pltpu.SemaphoreType.DMA((24,)),
        ],
        compiler_params=pltpu.CompilerParams(vmem_limit_bytes=VMEM_LIMIT),
        cost_estimate=pl.CostEstimate(flops=flops, bytes_accessed=8 << 20, transcendentals=0),
    )(place, *tokens, *weights, cosine, sine)


def attend_kernel(place, queries, kv0, kv1, kv2, kv3, mine, other, store, sems):
    ctx, x = place[0], place[1]
    rows = kv0.shape[1]
    handles = []
    for r, ref in enumerate((kv0, kv1, kv2, kv3)):
        for m in range(4):
            block = ctx ^ (4 * m + r)
            into = store.at[pl.ds(pl.multiple_of(block * rows, rows), rows)]
            handles.append(pltpu.make_async_copy(ref.at[m], into, sems.at[4 * r + m]))
    for handle in handles:
        handle.start()
    for handle in handles:
        handle.wait()
    z, e = ctx // 4, ctx % 4
    scale = 1.0 / math.sqrt(HEAD_SIZE)
    span = 4 * rows
    heads = queries.shape[1] // rows
    group = 2
    for block in range(4):
        count = (block + 1) * span
        slot = z ^ block
        keys, values = store[:count, :HEAD_SIZE], store[:count, HEAD_SIZE:]
        row = lax.broadcasted_iota(jnp.int32, (group * rows, span), 0) % rows + e * rows
        column = lax.broadcasted_iota(jnp.int32, (group * rows, span), 1)
        allowed = column <= row
        for first in range(0, heads, group):
            query = queries[slot, pl.ds(first * rows, group * rows), :]
            scores = lax.dot_general(
                query, keys, (((1,), (1,)), ((), ())), preferred_element_type=jnp.float32
            ) * jnp.float32(scale)
            last = jnp.where(allowed, scores[:, count - span :], jnp.float32(-1e30))
            scores = jnp.concatenate([scores[:, : count - span], last], axis=1) if block else last
            top = jnp.max(scores, axis=1, keepdims=True)
            weights = jnp.exp(scores - top)
            total = jnp.sum(weights, axis=1, keepdims=True)
            summed = jnp.dot(
                weights.astype(jnp.bfloat16), values, preferred_element_type=jnp.float32
            )
            normed = (summed / total).astype(jnp.bfloat16)
            for k in range(group):
                head = first + k
                piece = normed[k * rows : (k + 1) * rows]

                @pl.when(x == block // 2)
                def _():
                    mine[block % 2, :, head * HEAD_SIZE : (head + 1) * HEAD_SIZE] = piece

                @pl.when(x != block // 2)
                def _():
                    other[block % 2, :, head * HEAD_SIZE : (head + 1) * HEAD_SIZE] = piece


def attend(place, queries, kv):
    _, stacked, _ = queries.shape
    rows = kv[0].shape[1]
    heads = stacked // rows
    shape = jax.ShapeDtypeStruct((2, rows, heads * HEAD_SIZE), jnp.bfloat16)
    work = 4 * stacked * 16 * rows * HEAD_SIZE
    return pl.pallas_call(
        attend_kernel,
        out_shape=(shape, shape),
        in_specs=[smem_spec(), vmem_spec()] + any_specs(4),
        out_specs=(vmem_spec(), vmem_spec()),
        scratch_shapes=[
            pltpu.VMEM((16 * rows, 2 * HEAD_SIZE), jnp.bfloat16),
            pltpu.SemaphoreType.DMA((16,)),
        ],
        compiler_params=pltpu.CompilerParams(vmem_limit_bytes=VMEM_LIMIT),
        cost_estimate=pl.CostEstimate(
            flops=4 * work, bytes_accessed=4 << 20, transcendentals=4 * stacked * 16 * rows
        ),
    )(place, queries, *kv)


def output_kernel(place, *refs):
    attn_refs, weight_refs = refs[:8], refs[8:16]
    out0, out1, attn, wgt, sems = refs[16:]
    ctx, x = place[0], place[1]
    z, y, c = ctx // 4, ctx // 2 % 2, ctx % 2
    _, rows, width = attn_refs[0].shape
    depth, cols = weight_refs[0].shape
    handles = []
    for rx in range(2):
        for m in range(4):
            at = (x ^ rx) * depth + (z ^ m) * width
            into = attn.at[:, :, pl.ds(pl.multiple_of(at, width), width)]
            n = rx * 4 + m
            handles.append(pltpu.make_async_copy(attn_refs[n], into, sems.at[n]))
    for n in range(8):
        ry, rx, rc = n // 4, n // 2 % 2, n % 2
        at = ((y ^ ry) * 2 + (c ^ rc)) * cols
        into = wgt.at[
            pl.ds(pl.multiple_of((x ^ rx) * depth, depth), depth),
            pl.ds(pl.multiple_of(at, cols), cols),
        ]
        handles.append(pltpu.make_async_copy(weight_refs[n], into, sems.at[8 + n]))
    for handle in handles:
        handle.start()
    for handle in handles:
        handle.wait()
    low = z % 2
    for part in range(4):
        at = slice(part * cols, (part + 1) * cols)
        terms = []
        for f in range(2):
            term = jnp.dot(
                attn[:, :, f * depth : (f + 1) * depth].reshape(2 * rows, depth),
                wgt[f * depth : (f + 1) * depth, at],
                preferred_element_type=jnp.float32,
            )
            terms.append(term.astype(jnp.bfloat16).astype(jnp.float32))
        mixed = (terms[0] + terms[1]).astype(jnp.bfloat16)
        first, second = mixed[:rows], mixed[rows:]

        @pl.when(low == 0)
        def _():
            out0[:, at] = first
            out1[:, at] = second

        @pl.when(low == 1)
        def _():
            out0[:, at] = second
            out1[:, at] = first


def project_out(place, attn, weights):
    _, rows, width = attn[0].shape
    depth, cols = weights[0].shape
    shape = jax.ShapeDtypeStruct((rows, 4 * cols), jnp.bfloat16)
    return pl.pallas_call(
        output_kernel,
        out_shape=(shape, shape),
        in_specs=[smem_spec()] + any_specs(16),
        out_specs=(vmem_spec(), vmem_spec()),
        scratch_shapes=[
            pltpu.VMEM((2, rows, 2 * depth), jnp.bfloat16),
            pltpu.VMEM((2 * depth, 4 * cols), jnp.bfloat16),
            pltpu.SemaphoreType.DMA((16,)),
        ],
        compiler_params=pltpu.CompilerParams(vmem_limit_bytes=VMEM_LIMIT),
        cost_estimate=pl.CostEstimate(
            flops=2 * 2 * rows * 2 * depth * 4 * cols, bytes_accessed=12 << 20, transcendentals=0
        ),
    )(place, *attn, *weights)


def spread_weights(weight, z):
    width = weight.shape[1] // 4

    def piece(m):
        return lax.dynamic_slice_in_dim(weight, (z ^ m) * width, width, 1)

    own = jnp.stack([piece(0)] + [across_z(piece(m), m) for m in (1, 2, 3)])
    over_y = across_y(own)
    return [own, across_core(own), over_y, across_core(over_y)]


def split_body(tokens, w_query, key_matrix, value_matrix, w_out):
    ctx, x = lax.axis_index("ctx"), lax.axis_index("fsdp")
    place = jnp.stack([ctx, x]).astype(jnp.int32)
    z = ctx // 4
    rows = tokens.shape[0]

    head_major = jnp.concatenate(
        [
            key_matrix.reshape(-1, 4, HEAD_SIZE),
            value_matrix.reshape(-1, 4, HEAD_SIZE),
        ],
        axis=2,
    ).reshape(key_matrix.shape[0], -1)
    kv_weights = spread_weights(head_major, z)
    over_z = [tokens] + [across_z(tokens, m) for m in (1, 2, 3)]
    token_pieces = []
    for piece in over_z:
        token_pieces += [piece, across_x(piece)]

    slot = jnp.arange(4, dtype=jnp.int32)[:, None]
    positions = (ctx ^ (4 * slot)) * rows + jnp.arange(rows, dtype=jnp.int32)[None, :]
    cosine, sine = rotary_tables(positions.reshape(-1))
    cosine = jnp.concatenate([cosine, cosine], axis=1)
    sine = jnp.concatenate([-sine, sine], axis=1)

    own_kv = project(
        kv_kernel, (4, rows, 2 * HEAD_SIZE), place, token_pieces, kv_weights, cosine, sine
    )
    y_kv = across_y(own_kv)
    kv = [own_kv, across_core(own_kv), y_kv, across_core(y_kv)]

    query_weights = spread_weights(w_query, z)
    group = w_query.shape[1] // 4
    queries = project(
        query_kernel,
        (4, group // HEAD_SIZE * rows, HEAD_SIZE),
        place,
        token_pieces,
        query_weights,
        cosine,
        sine,
    )
    mine, other = attend(place, queries, kv)
    from_x = across_x(other)
    attn = [mine] + [across_z(mine, m) for m in (1, 2, 3)]
    attn += [from_x] + [across_z(from_x, m) for m in (1, 2, 3)]

    y_out = across_y(w_out)
    out_weights = []
    for piece in (w_out, across_x(w_out), y_out, across_x(y_out)):
        out_weights += [piece, across_core(piece)]
    first, second = project_out(place, attn, out_weights)

    def home(m):
        return lambda z, y, c, x: (2 * x + (z % 2 ^ m), y, c, z // 2)

    first, second = move(first, home(0)), move(second, home(1))
    odd = z % 2 == 1
    return jnp.concatenate(
        [jnp.where(odd, second, first), jnp.where(odd, first, second)], axis=1
    )


def solution(mesh):
    in_specs = (
        P("ctx", "fsdp"),
        P("ctx", "fsdp"),
        P("ctx", "fsdp"),
        P("ctx", "fsdp"),
        P("fsdp", "ctx"),
    )
    out_specs = P("ctx", "fsdp")
    split = mesh.shape["ctx"] == 16 and mesh.shape["fsdp"] == 2
    body = split_body if split else gathered_body
    return jax.shard_map(body, mesh=mesh, in_specs=in_specs, out_specs=out_specs, check_vma=False)
```

```python
import functools
import math

import jax
import jax.numpy as jnp
from jax import lax
from jax.experimental import pallas as pl
from jax.experimental.pallas import tpu as pltpu
from jax.sharding import PartitionSpec as P

HEAD_SIZE = 128
AXES = ("ctx", "fsdp")
VMEM_LIMIT = 18 * 1024 * 1024


def rotary_tables(positions):
    half_dim = HEAD_SIZE // 2
    inverse_freq = jnp.power(
        jnp.float32(500000.0), -jnp.arange(half_dim, dtype=jnp.float32) * 2.0 / HEAD_SIZE
    )
    angles = positions.astype(jnp.float32)[:, None] * inverse_freq[None, :]
    return jnp.cos(angles), jnp.sin(angles)


def rotate_heads(values, positions):
    tok_count = values.shape[0]
    head_count = values.shape[1] // HEAD_SIZE
    half_dim = HEAD_SIZE // 2
    cosine, sine_table = rotary_tables(positions)
    cosine, sine_table = cosine[:, None, :], sine_table[:, None, :]
    shaped = values.reshape(tok_count, head_count, HEAD_SIZE)
    first_half = shaped[:, :, :half_dim]
    second = shaped[:, :, half_dim:]
    turned = jnp.concatenate(
        [first_half * cosine - second * sine_table, second * cosine + first_half * sine_table],
        axis=2,
    )
    return turned.reshape(tok_count, head_count * HEAD_SIZE).astype(jnp.bfloat16)


def gathered_body(tokens, w_query, key_matrix, value_matrix, w_out):
    features = lax.all_gather(tokens, "fsdp", axis=1, tiled=True)
    tok_count = features.shape[0]
    positions = lax.axis_index("ctx") * tok_count + jnp.arange(tok_count, dtype=jnp.int32)

    def add_rows(weight_piece):
        return jnp.dot(features, weight_piece, preferred_element_type=jnp.float32)

    query_sum = add_rows(lax.all_gather(w_query, "ctx", axis=0, tiled=True))
    key_sum = add_rows(lax.all_gather(key_matrix, "ctx", axis=0, tiled=True))
    value_sum = add_rows(lax.all_gather(value_matrix, "ctx", axis=0, tiled=True))
    queries = rotate_heads(query_sum, positions)
    projected_keys = rotate_heads(key_sum, positions)
    projected_values = value_sum.astype(jnp.bfloat16)
    kv_heads = projected_keys.shape[1] // HEAD_SIZE
    queries_per_group = queries.shape[1] // projected_keys.shape[1]
    stacked = (
        queries.reshape(tok_count, kv_heads, queries_per_group, HEAD_SIZE)
        .transpose(1, 2, 0, 3)
        .reshape(kv_heads, queries_per_group * tok_count, HEAD_SIZE)
    )
    query_pos = jnp.tile(positions, queries_per_group)
    score_scale = 1.0 / math.sqrt(HEAD_SIZE)

    def update(attn_state, key_block, value_block, key_start):
        row_max, row_total, accum = attn_state
        block_rows = key_block.shape[0]
        key_heads = key_block.reshape(block_rows, kv_heads, HEAD_SIZE)
        value_heads = value_block.reshape(block_rows, kv_heads, HEAD_SIZE)
        scores = (
            jnp.einsum("gqd,kgd->gqk", stacked, key_heads, preferred_element_type=jnp.float32)
            * score_scale
        )
        key_pos = key_start + jnp.arange(block_rows, dtype=jnp.int32)
        allowed = (key_pos[None, :] <= query_pos[:, None])[None]
        masked = jnp.where(allowed, scores, jnp.float32(-1e30))
        new_max = jnp.maximum(row_max, jnp.max(masked, axis=2))
        exp_weights = jnp.where(allowed, jnp.exp(masked - new_max[:, :, None]), jnp.float32(0.0))
        factor = jnp.exp(row_max - new_max)
        row_total = row_total * factor + jnp.sum(exp_weights, axis=2)
        accum = accum * factor[:, :, None] + jnp.einsum(
            "gqk,kgd->gqd",
            exp_weights.astype(jnp.bfloat16),
            value_heads,
            preferred_element_type=jnp.float32,
        )
        return (new_max, row_total, accum)

    query_rows = queries_per_group * tok_count
    initial = (
        jnp.full((kv_heads, query_rows), -1e30, jnp.float32),
        jnp.zeros((kv_heads, query_rows), jnp.float32),
        jnp.zeros((kv_heads, query_rows, HEAD_SIZE), jnp.float32),
    )
    key_piece = lax.all_gather(projected_keys, "ctx", axis=0, tiled=True)
    value_piece = lax.all_gather(projected_values, "ctx", axis=0, tiled=True)
    block_rows = min(tok_count, key_piece.shape[0])
    block_count = key_piece.shape[0] // block_rows

    def advance(block_index, carried):
        key_start = block_index * block_rows
        key_block = lax.dynamic_slice_in_dim(key_piece, block_index * block_rows, block_rows, 0)
        value_block = lax.dynamic_slice_in_dim(value_piece, block_index * block_rows, block_rows, 0)
        return update(carried, key_block, value_block, key_start)

    row_max, row_total, accum = lax.fori_loop(0, block_count, advance, initial)
    normed = accum / row_total[:, :, None]
    attn_out = (
        normed.reshape(kv_heads, queries_per_group, tok_count, HEAD_SIZE)
        .transpose(2, 0, 1, 3)
        .reshape(tok_count, kv_heads * queries_per_group * HEAD_SIZE)
        .astype(jnp.bfloat16)
    )
    partial_out = jnp.dot(
        attn_out,
        lax.all_gather(w_out, "ctx", axis=1, tiled=True),
        preferred_element_type=jnp.float32,
    )
    return lax.psum_scatter(
        partial_out.astype(jnp.bfloat16), "fsdp", scatter_dimension=1, tiled=True
    )


def moves(target):
    pairs = []
    for i in range(32):
        z, y, c, x = i // 8, i // 4 % 2, i // 2 % 2, i % 2
        tz, ty, tc, tx = target(z, y, c, x)
        pairs.append((i, tz * 8 + ty * 4 + tc * 2 + tx))
    return pairs


def move(array, target):
    return lax.ppermute(array, AXES, moves(target))


def across_z(array, m):
    return move(array, lambda z, y, c, x: (z ^ m, y, c, x))


def across_y(array):
    return move(array, lambda z, y, c, x: (z, 1 - y, c, x))


def across_core(array):
    return move(array, lambda z, y, c, x: (z, y, 1 - c, x))


def across_x(array):
    return move(array, lambda z, y, c, x: (z, y, c, 1 - x))


def any_specs(count):
    return [pl.BlockSpec(memory_space=pl.ANY)] * count


def smem_spec():
    return pl.BlockSpec(memory_space=pltpu.SMEM)


def vmem_spec():
    return pl.BlockSpec(memory_space=pltpu.VMEM)


def load_projection(place, token_refs, weight_refs, plan, first_column, tok, wgt, sems):
    ctx, x = place[0], place[1]
    rows, half = token_refs[0].shape
    depth, width = wgt.shape[0] // 16, wgt.shape[1]
    copies = []
    for m in range(4):
        for rx in range(2):
            into = tok.at[pl.ds(m * rows, rows), pl.ds(pl.multiple_of((x ^ rx) * half, half), half)]
            copies.append((token_refs[m * 2 + rx], into))
    for ref, blocks in zip(weight_refs, plan, strict=True):
        at = first_column if ref.shape[-1] > width else 0
        for k, relative in enumerate(blocks):
            into = wgt.at[pl.ds(pl.multiple_of((ctx ^ relative) * depth, depth), depth)]
            copies.append((ref.at[k, :, pl.ds(at, width)], into))
    handles = [pltpu.make_async_copy(s, d, sems.at[i]) for i, (s, d) in enumerate(copies)]
    for handle in handles:
        handle.start()
    for handle in handles:
        handle.wait()


def rotated(values, cosine, sine):
    turned = jnp.concatenate([values[:, HEAD_SIZE // 2 :], values[:, : HEAD_SIZE // 2]], axis=1)
    return values * cosine + turned * sine


def kv_kernel(plan, place, *refs):
    token_refs, weight_refs = refs[:8], refs[8:-6]
    cosine, sine, out, tok, wgt, sems = refs[-6:]
    load_projection(place, token_refs, weight_refs, plan, 0, tok, wgt, sems)
    rows = tok.shape[0] // 4
    values = jnp.dot(tok[...], wgt[...], preferred_element_type=jnp.float32)
    keys = rotated(values[:, :HEAD_SIZE], cosine[...], sine[...]).astype(jnp.bfloat16)
    vals = values[:, HEAD_SIZE:].astype(jnp.bfloat16)
    for m in range(4):
        out[m, :, :HEAD_SIZE] = keys[m * rows : (m + 1) * rows]
        out[m, :, HEAD_SIZE:] = vals[m * rows : (m + 1) * rows]


def query_kernel(plan, place, *refs):
    token_refs, weight_refs = refs[:8], refs[8:-6]
    cosine, sine, out, tok, wgt, sems = refs[-6:]
    load_projection(place, token_refs, weight_refs, plan, 2 * HEAD_SIZE, tok, wgt, sems)
    rows = tok.shape[0] // 4
    heads = wgt.shape[1] // HEAD_SIZE
    for pair in range(heads // 2):
        values = jnp.dot(
            tok[...],
            wgt[:, pair * 2 * HEAD_SIZE : (pair + 1) * 2 * HEAD_SIZE],
            preferred_element_type=jnp.float32,
        )
        for k in range(2):
            one = rotated(values[:, k * HEAD_SIZE : (k + 1) * HEAD_SIZE], cosine[...], sine[...])
            one = one.astype(jnp.bfloat16)
            head = pair * 2 + k
            for m in range(4):
                out[m, head * rows : (head + 1) * rows, :] = one[m * rows : (m + 1) * rows]


def project(kernel, out_shape, place, tokens, weights, plan, width, cosine, sine):
    rows, half = tokens[0].shape
    depth = weights[0].shape[1]
    flops = 16 * 4 * rows * 16 * depth * HEAD_SIZE * 4
    return pl.pallas_call(
        functools.partial(kernel, plan),
        out_shape=jax.ShapeDtypeStruct(out_shape, jnp.bfloat16),
        in_specs=[smem_spec()] + any_specs(8 + len(weights)) + [vmem_spec()] * 2,
        out_specs=vmem_spec(),
        scratch_shapes=[
            pltpu.VMEM((4 * rows, 2 * half), jnp.bfloat16),
            pltpu.VMEM((16 * depth, width), jnp.bfloat16),
            pltpu.SemaphoreType.DMA((24,)),
        ],
        compiler_params=pltpu.CompilerParams(vmem_limit_bytes=VMEM_LIMIT),
        cost_estimate=pl.CostEstimate(flops=flops, bytes_accessed=8 << 20, transcendentals=0),
    )(place, *tokens, *weights, cosine, sine)


def attend_kernel(place, queries, kv0, kv1, kv2, kv3, mine, other, store, sems):
    ctx, x = place[0], place[1]
    rows = kv0.shape[1]
    handles = []
    for r, ref in enumerate((kv0, kv1, kv2, kv3)):
        for m in range(4):
            block = ctx ^ (4 * m + r)
            into = store.at[pl.ds(pl.multiple_of(block * rows, rows), rows)]
            handles.append(pltpu.make_async_copy(ref.at[m], into, sems.at[4 * r + m]))
    for handle in handles:
        handle.start()
    for handle in handles:
        handle.wait()
    z, e = ctx // 4, ctx % 4
    scale = 1.0 / math.sqrt(HEAD_SIZE)
    span = 4 * rows
    heads = queries.shape[1] // rows
    group = 2
    for block in range(4):
        count = (block + 1) * span
        slot = z ^ block
        keys, values = store[:count, :HEAD_SIZE], store[:count, HEAD_SIZE:]
        row = lax.broadcasted_iota(jnp.int32, (group * rows, span), 0) % rows + e * rows
        column = lax.broadcasted_iota(jnp.int32, (group * rows, span), 1)
        allowed = column <= row
        for first in range(0, heads, group):
            query = queries[slot, pl.ds(first * rows, group * rows), :]
            scores = lax.dot_general(
                query, keys, (((1,), (1,)), ((), ())), preferred_element_type=jnp.float32
            ) * jnp.float32(scale)
            last = jnp.where(allowed, scores[:, count - span :], jnp.float32(-1e30))
            scores = jnp.concatenate([scores[:, : count - span], last], axis=1) if block else last
            top = jnp.max(scores, axis=1, keepdims=True)
            weights = jnp.exp(scores - top)
            total = jnp.sum(weights, axis=1, keepdims=True)
            summed = jnp.dot(
                weights.astype(jnp.bfloat16), values, preferred_element_type=jnp.float32
            )
            normed = (summed / total).astype(jnp.bfloat16)
            for k in range(group):
                head = first + k
                piece = normed[k * rows : (k + 1) * rows]

                @pl.when(x == block // 2)
                def _():
                    mine[block % 2, :, head * HEAD_SIZE : (head + 1) * HEAD_SIZE] = piece

                @pl.when(x != block // 2)
                def _():
                    other[block % 2, :, head * HEAD_SIZE : (head + 1) * HEAD_SIZE] = piece


def attend(place, queries, kv):
    _, stacked, _ = queries.shape
    rows = kv[0].shape[1]
    heads = stacked // rows
    shape = jax.ShapeDtypeStruct((2, rows, heads * HEAD_SIZE), jnp.bfloat16)
    work = 4 * stacked * 16 * rows * HEAD_SIZE
    return pl.pallas_call(
        attend_kernel,
        out_shape=(shape, shape),
        in_specs=[smem_spec(), vmem_spec()] + any_specs(4),
        out_specs=(vmem_spec(), vmem_spec()),
        scratch_shapes=[
            pltpu.VMEM((16 * rows, 2 * HEAD_SIZE), jnp.bfloat16),
            pltpu.SemaphoreType.DMA((16,)),
        ],
        compiler_params=pltpu.CompilerParams(vmem_limit_bytes=VMEM_LIMIT),
        cost_estimate=pl.CostEstimate(
            flops=20 * work, bytes_accessed=4 << 20, transcendentals=4 * stacked * 16 * rows
        ),
    )(place, queries, *kv)


def output_kernel(place, *refs):
    attn_refs, weight_refs = refs[:8], refs[8:16]
    out0, out1, attn, wgt, sems = refs[16:]
    ctx, x = place[0], place[1]
    z, y, c = ctx // 4, ctx // 2 % 2, ctx % 2
    _, rows, width = attn_refs[0].shape
    depth, cols = weight_refs[0].shape
    handles = []
    for rx in range(2):
        for m in range(4):
            at = (x ^ rx) * depth + (z ^ m) * width
            into = attn.at[:, :, pl.ds(pl.multiple_of(at, width), width)]
            n = rx * 4 + m
            handles.append(pltpu.make_async_copy(attn_refs[n], into, sems.at[n]))
    for n in range(8):
        ry, rx, rc = n // 4, n // 2 % 2, n % 2
        at = ((y ^ ry) * 2 + (c ^ rc)) * cols
        into = wgt.at[
            pl.ds(pl.multiple_of((x ^ rx) * depth, depth), depth),
            pl.ds(pl.multiple_of(at, cols), cols),
        ]
        handles.append(pltpu.make_async_copy(weight_refs[n], into, sems.at[8 + n]))
    for handle in handles:
        handle.start()
    for handle in handles:
        handle.wait()
    low = z % 2
    for part in range(4):
        at = slice(part * cols, (part + 1) * cols)
        terms = []
        for f in range(2):
            term = jnp.dot(
                attn[:, :, f * depth : (f + 1) * depth].reshape(2 * rows, depth),
                wgt[f * depth : (f + 1) * depth, at],
                preferred_element_type=jnp.float32,
            )
            terms.append(term.astype(jnp.bfloat16).astype(jnp.float32))
        mixed = (terms[0] + terms[1]).astype(jnp.bfloat16)
        first, second = mixed[:rows], mixed[rows:]

        @pl.when(low == 0)
        def _():
            out0[:, at] = first
            out1[:, at] = second

        @pl.when(low == 1)
        def _():
            out0[:, at] = second
            out1[:, at] = first


def project_out(place, attn, weights):
    _, rows, width = attn[0].shape
    depth, cols = weights[0].shape
    shape = jax.ShapeDtypeStruct((rows, 4 * cols), jnp.bfloat16)
    return pl.pallas_call(
        output_kernel,
        out_shape=(shape, shape),
        in_specs=[smem_spec()] + any_specs(16),
        out_specs=(vmem_spec(), vmem_spec()),
        scratch_shapes=[
            pltpu.VMEM((2, rows, 2 * depth), jnp.bfloat16),
            pltpu.VMEM((2 * depth, 4 * cols), jnp.bfloat16),
            pltpu.SemaphoreType.DMA((16,)),
        ],
        compiler_params=pltpu.CompilerParams(vmem_limit_bytes=VMEM_LIMIT),
        cost_estimate=pl.CostEstimate(
            flops=2 * 2 * rows * 2 * depth * 4 * cols, bytes_accessed=12 << 20, transcendentals=0
        ),
    )(place, *attn, *weights)


def after(array, *earlier):
    return lax.optimization_barrier((array,) + earlier)[0]


def split_body(tokens, w_query, key_matrix, value_matrix, w_out):
    ctx, x = lax.axis_index("ctx"), lax.axis_index("fsdp")
    place = jnp.stack([ctx, x]).astype(jnp.int32)
    z = ctx // 4
    rows = tokens.shape[0]
    group = w_query.shape[1] // 4

    def columns(weight, head, width):
        return lax.dynamic_slice_in_dim(weight, head * width, width, 1)

    def pair(head):
        parts = [columns(w, head, HEAD_SIZE) for w in (key_matrix, value_matrix)]
        return jnp.concatenate(parts, axis=1)

    wide = 2 * HEAD_SIZE

    tok1 = across_z(tokens, 1)
    tok2 = across_z(tokens, 2)
    other0 = across_x(tokens)
    x_out = across_x(w_out)
    own = jnp.concatenate([pair(z), columns(w_query, z, group)], axis=1)
    own_y = across_y(own)
    y_out = across_y(after(w_out, own_y))
    far_half = [columns(w, 1 - z // 2, wide) for w in (key_matrix, value_matrix)]
    far = across_z(after(jnp.concatenate(far_half, axis=1), tok1, other0, own_y), 2)

    def far_pair(head):
        parts = [columns(w, head, HEAD_SIZE) for w in (far[:, :wide], far[:, wide:])]
        return jnp.concatenate(parts, axis=1)

    other1 = across_x(after(tok1, other0, own_y))
    tok3 = across_z(after(tok2, tok1, x_out, own_y), 1)
    xy_out = across_y(after(x_out, own_y))
    other2 = across_x(after(tok2, other1))
    near = across_z(after(jnp.stack([pair(z ^ 1), far_pair(1 - z % 2)]), y_out), 1)
    query2 = across_z(after(columns(w_query, z ^ 2, group), far), 2)
    query3 = across_z(after(columns(w_query, z ^ 3, group), far, tok3, other1), 3)
    other3 = across_x(after(tok3, other1))
    query1 = across_z(after(columns(w_query, z ^ 1, group), far, near), 1)
    token_pieces = [tokens, other0, tok1, other1, tok2, other2, tok3, other3]

    both = jnp.stack([own, own_y])
    both_core = across_core(after(both, other1))
    kv_rest = jnp.stack([near[0], far_pair(z % 2), near[1]])
    kv_rest_y = across_y(after(kv_rest, both_core, y_out, xy_out, other2))
    query2_y = across_y(after(query2, kv_rest_y))
    query31_y = across_y(after(jnp.stack([query3, query1]), kv_rest_y))
    kv_core = across_core(after(jnp.concatenate([kv_rest, kv_rest_y]), other3))
    kv_weights = [both, both_core, kv_rest, kv_rest_y, kv_core]
    kv_plan = ((0, 2), (1, 3), (4, 8, 12), (6, 10, 14), (5, 9, 13, 7, 11, 15))

    slot = jnp.arange(4, dtype=jnp.int32)[:, None]
    positions = (ctx ^ (4 * slot)) * rows + jnp.arange(rows, dtype=jnp.int32)[None, :]
    cosine, sine = rotary_tables(positions.reshape(-1))
    cosine = jnp.concatenate([cosine, cosine], axis=1)
    sine = jnp.concatenate([-sine, sine], axis=1)

    own_kv = project(
        kv_kernel,
        (4, rows, wide),
        place,
        token_pieces,
        kv_weights,
        kv_plan,
        wide,
        cosine,
        sine,
    )
    y_kv = across_y(own_kv)
    kv = [own_kv, across_core(own_kv), y_kv, across_core(y_kv)]
    query_rest = jnp.stack([query1, query2, query3, query31_y[1], query2_y, query31_y[0]])
    query_core = across_core(after(query_rest, own_kv))
    query_weights = [both, both_core, query_rest, query_core]
    query_plan = ((0, 2), (1, 3), (4, 8, 12, 6, 10, 14), (5, 9, 13, 7, 11, 15))
    queries = project(
        query_kernel,
        (4, group // HEAD_SIZE * rows, HEAD_SIZE),
        place,
        token_pieces,
        query_weights,
        query_plan,
        group,
        cosine,
        sine,
    )
    mine, other = attend(place, queries, kv)
    out_weights = []
    for piece in (w_out, x_out, y_out, xy_out):
        out_weights += [piece, across_core(piece)]
    mine, other = after(mine, *out_weights), after(other, *out_weights)
    mine2 = across_z(mine, 2)
    mine1 = across_z(mine, 1)
    from_x = across_x(other)
    from_x2 = across_z(from_x, 2)
    from_x1 = across_z(after(from_x, mine1), 1)
    mine3 = across_z(mine2, 1)
    from_x3 = across_z(from_x2, 1)
    attn = [mine, mine1, mine2, mine3, from_x, from_x1, from_x2, from_x3]

    first, second = project_out(place, attn, out_weights)

    def home(m):
        return lambda z, y, c, x: (2 * x + (z % 2 ^ m), y, c, z // 2)

    first, second = move(first, home(0)), move(second, home(1))
    odd = z % 2 == 1
    return jnp.concatenate(
        [jnp.where(odd, second, first), jnp.where(odd, first, second)], axis=1
    )


def solution(mesh):
    in_specs = (
        P("ctx", "fsdp"),
        P("ctx", "fsdp"),
        P("ctx", "fsdp"),
        P("ctx", "fsdp"),
        P("fsdp", "ctx"),
    )
    out_specs = P("ctx", "fsdp")
    split = mesh.shape["ctx"] == 16 and mesh.shape["fsdp"] == 2
    body = split_body if split else gathered_body
    return jax.shard_map(body, mesh=mesh, in_specs=in_specs, out_specs=out_specs, check_vma=False)
```

```python
import functools
import math

import jax
import jax.numpy as jnp
from jax import lax
from jax.experimental import pallas as pl
from jax.experimental.pallas import tpu as pltpu
from jax.sharding import PartitionSpec as P

HEAD_SIZE = 128
AXES = ("ctx", "fsdp")
VMEM_LIMIT = 18 * 1024 * 1024


def rotary_tables(positions):
    half_dim = HEAD_SIZE // 2
    inverse_freq = jnp.power(
        jnp.float32(500000.0), -jnp.arange(half_dim, dtype=jnp.float32) * 2.0 / HEAD_SIZE
    )
    angles = positions.astype(jnp.float32)[:, None] * inverse_freq[None, :]
    return jnp.cos(angles), jnp.sin(angles)


def rotate_heads(values, positions):
    tok_count = values.shape[0]
    head_count = values.shape[1] // HEAD_SIZE
    half_dim = HEAD_SIZE // 2
    cosine, sine_table = rotary_tables(positions)
    cosine, sine_table = cosine[:, None, :], sine_table[:, None, :]
    shaped = values.reshape(tok_count, head_count, HEAD_SIZE)
    first_half = shaped[:, :, :half_dim]
    second = shaped[:, :, half_dim:]
    turned = jnp.concatenate(
        [first_half * cosine - second * sine_table, second * cosine + first_half * sine_table],
        axis=2,
    )
    return turned.reshape(tok_count, head_count * HEAD_SIZE).astype(jnp.bfloat16)


def gathered_body(tokens, w_query, key_matrix, value_matrix, w_out):
    features = lax.all_gather(tokens, "fsdp", axis=1, tiled=True)
    tok_count = features.shape[0]
    positions = lax.axis_index("ctx") * tok_count + jnp.arange(tok_count, dtype=jnp.int32)

    def add_rows(weight_piece):
        return jnp.dot(features, weight_piece, preferred_element_type=jnp.float32)

    query_sum = add_rows(lax.all_gather(w_query, "ctx", axis=0, tiled=True))
    key_sum = add_rows(lax.all_gather(key_matrix, "ctx", axis=0, tiled=True))
    value_sum = add_rows(lax.all_gather(value_matrix, "ctx", axis=0, tiled=True))
    queries = rotate_heads(query_sum, positions)
    projected_keys = rotate_heads(key_sum, positions)
    projected_values = value_sum.astype(jnp.bfloat16)
    kv_heads = projected_keys.shape[1] // HEAD_SIZE
    queries_per_group = queries.shape[1] // projected_keys.shape[1]
    stacked = (
        queries.reshape(tok_count, kv_heads, queries_per_group, HEAD_SIZE)
        .transpose(1, 2, 0, 3)
        .reshape(kv_heads, queries_per_group * tok_count, HEAD_SIZE)
    )
    query_pos = jnp.tile(positions, queries_per_group)
    score_scale = 1.0 / math.sqrt(HEAD_SIZE)

    def update(attn_state, key_block, value_block, key_start):
        row_max, row_total, accum = attn_state
        block_rows = key_block.shape[0]
        key_heads = key_block.reshape(block_rows, kv_heads, HEAD_SIZE)
        value_heads = value_block.reshape(block_rows, kv_heads, HEAD_SIZE)
        scores = (
            jnp.einsum("gqd,kgd->gqk", stacked, key_heads, preferred_element_type=jnp.float32)
            * score_scale
        )
        key_pos = key_start + jnp.arange(block_rows, dtype=jnp.int32)
        allowed = (key_pos[None, :] <= query_pos[:, None])[None]
        masked = jnp.where(allowed, scores, jnp.float32(-1e30))
        new_max = jnp.maximum(row_max, jnp.max(masked, axis=2))
        exp_weights = jnp.where(allowed, jnp.exp(masked - new_max[:, :, None]), jnp.float32(0.0))
        factor = jnp.exp(row_max - new_max)
        row_total = row_total * factor + jnp.sum(exp_weights, axis=2)
        accum = accum * factor[:, :, None] + jnp.einsum(
            "gqk,kgd->gqd",
            exp_weights.astype(jnp.bfloat16),
            value_heads,
            preferred_element_type=jnp.float32,
        )
        return (new_max, row_total, accum)

    query_rows = queries_per_group * tok_count
    initial = (
        jnp.full((kv_heads, query_rows), -1e30, jnp.float32),
        jnp.zeros((kv_heads, query_rows), jnp.float32),
        jnp.zeros((kv_heads, query_rows, HEAD_SIZE), jnp.float32),
    )
    key_piece = lax.all_gather(projected_keys, "ctx", axis=0, tiled=True)
    value_piece = lax.all_gather(projected_values, "ctx", axis=0, tiled=True)
    block_rows = min(tok_count, key_piece.shape[0])
    block_count = key_piece.shape[0] // block_rows

    def advance(block_index, carried):
        key_start = block_index * block_rows
        key_block = lax.dynamic_slice_in_dim(key_piece, block_index * block_rows, block_rows, 0)
        value_block = lax.dynamic_slice_in_dim(value_piece, block_index * block_rows, block_rows, 0)
        return update(carried, key_block, value_block, key_start)

    row_max, row_total, accum = lax.fori_loop(0, block_count, advance, initial)
    normed = accum / row_total[:, :, None]
    attn_out = (
        normed.reshape(kv_heads, queries_per_group, tok_count, HEAD_SIZE)
        .transpose(2, 0, 1, 3)
        .reshape(tok_count, kv_heads * queries_per_group * HEAD_SIZE)
        .astype(jnp.bfloat16)
    )
    partial_out = jnp.dot(
        attn_out,
        lax.all_gather(w_out, "ctx", axis=1, tiled=True),
        preferred_element_type=jnp.float32,
    )
    return lax.psum_scatter(
        partial_out.astype(jnp.bfloat16), "fsdp", scatter_dimension=1, tiled=True
    )


def moves(target):
    pairs = []
    for i in range(32):
        z, y, c, x = i // 8, i // 4 % 2, i // 2 % 2, i % 2
        tz, ty, tc, tx = target(z, y, c, x)
        pairs.append((i, tz * 8 + ty * 4 + tc * 2 + tx))
    return pairs


def move(array, target):
    return lax.ppermute(array, AXES, moves(target))


def across_z(array, m):
    return move(array, lambda z, y, c, x: (z ^ m, y, c, x))


def across_y(array):
    return move(array, lambda z, y, c, x: (z, 1 - y, c, x))


def across_core(array):
    return move(array, lambda z, y, c, x: (z, y, 1 - c, x))


def across_x(array):
    return move(array, lambda z, y, c, x: (z, y, c, 1 - x))


def any_specs(count):
    return [pl.BlockSpec(memory_space=pl.ANY)] * count


def smem_spec():
    return pl.BlockSpec(memory_space=pltpu.SMEM)


def vmem_spec():
    return pl.BlockSpec(memory_space=pltpu.VMEM)


def load_projection(place, token_refs, weight_refs, plan, first_column, tok, wgt, sems):
    ctx, x = place[0], place[1]
    rows, half = token_refs[0].shape
    depth, width = wgt.shape[0] // 16, wgt.shape[1]
    copies = []
    for m in range(4):
        for rx in range(2):
            into = tok.at[pl.ds(m * rows, rows), pl.ds(pl.multiple_of((x ^ rx) * half, half), half)]
            copies.append((token_refs[m * 2 + rx], into))
    for ref, blocks in zip(weight_refs, plan, strict=True):
        at = first_column if ref.shape[-1] > width else 0
        for k, relative in enumerate(blocks):
            into = wgt.at[pl.ds(pl.multiple_of((ctx ^ relative) * depth, depth), depth)]
            copies.append((ref.at[k, :, pl.ds(at, width)], into))
    handles = [pltpu.make_async_copy(s, d, sems.at[i]) for i, (s, d) in enumerate(copies)]
    for handle in handles:
        handle.start()
    for handle in handles:
        handle.wait()


def rotated(values, cosine, sine):
    turned = jnp.concatenate([values[:, HEAD_SIZE // 2 :], values[:, : HEAD_SIZE // 2]], axis=1)
    return values * cosine + turned * sine


def kv_kernel(plan, place, *refs):
    token_refs, weight_refs = refs[:8], refs[8:-6]
    cosine, sine, out, tok, wgt, sems = refs[-6:]
    load_projection(place, token_refs, weight_refs, plan, 0, tok, wgt, sems)
    rows = tok.shape[0] // 4
    values = jnp.dot(tok[...], wgt[...], preferred_element_type=jnp.float32)
    keys = rotated(values[:, :HEAD_SIZE], cosine[...], sine[...]).astype(jnp.bfloat16)
    vals = values[:, HEAD_SIZE:].astype(jnp.bfloat16)
    for m in range(4):
        out[m, :, :HEAD_SIZE] = keys[m * rows : (m + 1) * rows]
        out[m, :, HEAD_SIZE:] = vals[m * rows : (m + 1) * rows]


def query_kernel(plan, place, *refs):
    token_refs, weight_refs = refs[:8], refs[8:-6]
    cosine, sine, out, tok, wgt, sems = refs[-6:]
    load_projection(place, token_refs, weight_refs, plan, 2 * HEAD_SIZE, tok, wgt, sems)
    rows = tok.shape[0] // 4
    heads = wgt.shape[1] // HEAD_SIZE
    for pair in range(heads // 2):
        values = jnp.dot(
            tok[...],
            wgt[:, pair * 2 * HEAD_SIZE : (pair + 1) * 2 * HEAD_SIZE],
            preferred_element_type=jnp.float32,
        )
        for k in range(2):
            one = rotated(values[:, k * HEAD_SIZE : (k + 1) * HEAD_SIZE], cosine[...], sine[...])
            one = one.astype(jnp.bfloat16)
            head = pair * 2 + k
            for m in range(4):
                out[m, head * rows : (head + 1) * rows, :] = one[m * rows : (m + 1) * rows]


def project(kernel, out_shape, place, tokens, weights, plan, width, cosine, sine):
    rows, half = tokens[0].shape
    depth = weights[0].shape[1]
    flops = 16 * 4 * rows * 16 * depth * HEAD_SIZE * 4
    return pl.pallas_call(
        functools.partial(kernel, plan),
        out_shape=jax.ShapeDtypeStruct(out_shape, jnp.bfloat16),
        in_specs=[smem_spec()] + any_specs(8 + len(weights)) + [vmem_spec()] * 2,
        out_specs=vmem_spec(),
        scratch_shapes=[
            pltpu.VMEM((4 * rows, 2 * half), jnp.bfloat16),
            pltpu.VMEM((16 * depth, width), jnp.bfloat16),
            pltpu.SemaphoreType.DMA((24,)),
        ],
        compiler_params=pltpu.CompilerParams(vmem_limit_bytes=VMEM_LIMIT),
        cost_estimate=pl.CostEstimate(flops=flops, bytes_accessed=8 << 20, transcendentals=0),
    )(place, *tokens, *weights, cosine, sine)


def attend_kernel(place, queries, kv0, kv1, kv2, kv3, mine, other, store, sems):
    ctx, x = place[0], place[1]
    rows = kv0.shape[1]
    handles = []
    for r, ref in enumerate((kv0, kv1, kv2, kv3)):
        for m in range(4):
            block = ctx ^ (4 * m + r)
            into = store.at[pl.ds(pl.multiple_of(block * rows, rows), rows)]
            handles.append(pltpu.make_async_copy(ref.at[m], into, sems.at[4 * r + m]))
    for handle in handles:
        handle.start()
    for handle in handles:
        handle.wait()
    z, e = ctx // 4, ctx % 4
    scale = math.log2(math.e) / math.sqrt(HEAD_SIZE)
    span = 4 * rows
    heads = queries.shape[1] // rows
    group = 2
    row = lax.broadcasted_iota(jnp.int32, (group * rows, span), 0) % rows + e * rows
    column = lax.broadcasted_iota(jnp.int32, (group * rows, span), 1)
    allowed = column <= row

    def block_of(block, out):
        count = (block + 1) * span
        keys, values = store[:count, :HEAD_SIZE], store[:count, HEAD_SIZE:]
        for first in range(0, heads, group):
            query = queries[z ^ block, pl.ds(first * rows, group * rows), :]
            scores = lax.dot_general(
                query, keys, (((1,), (1,)), ((), ())), preferred_element_type=jnp.float32
            )
            last = jnp.where(allowed, scores[:, count - span :], jnp.float32(-1e30))
            scores = jnp.concatenate([scores[:, : count - span], last], axis=1) if block else last
            top = jnp.max(scores, axis=1, keepdims=True)
            weights = jnp.exp2((scores - top) * jnp.float32(scale))
            total = jnp.sum(weights, axis=1, keepdims=True)
            summed = jnp.dot(
                weights.astype(jnp.bfloat16), values, preferred_element_type=jnp.float32
            )
            normed = (summed / total).astype(jnp.bfloat16)
            for k in range(group):
                at = slice((first + k) * HEAD_SIZE, (first + k + 1) * HEAD_SIZE)
                out[block // 2, :, at] = normed[k * rows : (k + 1) * rows]

    @pl.when(x == 0)
    def _():
        for block in range(4):
            block_of(block, mine if block in (0, 3) else other)

    @pl.when(x == 1)
    def _():
        for block in range(4):
            block_of(block, mine if block in (1, 2) else other)


def attend(place, queries, kv):
    _, stacked, _ = queries.shape
    rows = kv[0].shape[1]
    heads = stacked // rows
    shape = jax.ShapeDtypeStruct((2, rows, heads * HEAD_SIZE), jnp.bfloat16)
    work = 4 * stacked * 16 * rows * HEAD_SIZE
    return pl.pallas_call(
        attend_kernel,
        out_shape=(shape, shape),
        in_specs=[smem_spec(), vmem_spec()] + any_specs(4),
        out_specs=(vmem_spec(), vmem_spec()),
        scratch_shapes=[
            pltpu.VMEM((16 * rows, 2 * HEAD_SIZE), jnp.bfloat16),
            pltpu.SemaphoreType.DMA((16,)),
        ],
        compiler_params=pltpu.CompilerParams(vmem_limit_bytes=VMEM_LIMIT),
        cost_estimate=pl.CostEstimate(
            flops=20 * work, bytes_accessed=4 << 20, transcendentals=4 * stacked * 16 * rows
        ),
    )(place, queries, *kv)


def output_kernel(place, *refs):
    attn_refs, weight_refs = refs[:8], refs[8:16]
    out0, out1, attn, wgt, sems = refs[16:]
    ctx, x = place[0], place[1]
    z, y, c = ctx // 4, ctx // 2 % 2, ctx % 2
    _, rows, width = attn_refs[0].shape
    depth, cols = weight_refs[0].shape
    handles = []
    for rx in range(2):
        for m in range(4):
            at = (x ^ rx) * depth + (z ^ m) * width
            into = attn.at[:, :, pl.ds(pl.multiple_of(at, width), width)]
            n = rx * 4 + m
            handles.append(pltpu.make_async_copy(attn_refs[n], into, sems.at[n]))
    for n in range(8):
        ry, rx, rc = n // 4, n // 2 % 2, n % 2
        at = ((y ^ ry) * 2 + (c ^ rc)) * cols
        into = wgt.at[
            pl.ds(pl.multiple_of((x ^ rx) * depth, depth), depth),
            pl.ds(pl.multiple_of(at, cols), cols),
        ]
        handles.append(pltpu.make_async_copy(weight_refs[n], into, sems.at[8 + n]))
    for handle in handles:
        handle.start()
    for handle in handles:
        handle.wait()
    low = z % 2
    for part in range(4):
        at = slice(part * cols, (part + 1) * cols)
        terms = []
        for f in range(2):
            term = jnp.dot(
                attn[:, :, f * depth : (f + 1) * depth].reshape(2 * rows, depth),
                wgt[f * depth : (f + 1) * depth, at],
                preferred_element_type=jnp.float32,
            )
            terms.append(term.astype(jnp.bfloat16).astype(jnp.float32))
        mixed = (terms[0] + terms[1]).astype(jnp.bfloat16)
        first, second = mixed[:rows], mixed[rows:]

        @pl.when(low == 0)
        def _():
            out0[:, at] = first
            out1[:, at] = second

        @pl.when(low == 1)
        def _():
            out0[:, at] = second
            out1[:, at] = first


def project_out(place, attn, weights):
    _, rows, width = attn[0].shape
    depth, cols = weights[0].shape
    shape = jax.ShapeDtypeStruct((rows, 4 * cols), jnp.bfloat16)
    return pl.pallas_call(
        output_kernel,
        out_shape=(shape, shape),
        in_specs=[smem_spec()] + any_specs(16),
        out_specs=(vmem_spec(), vmem_spec()),
        scratch_shapes=[
            pltpu.VMEM((2, rows, 2 * depth), jnp.bfloat16),
            pltpu.VMEM((2 * depth, 4 * cols), jnp.bfloat16),
            pltpu.SemaphoreType.DMA((16,)),
        ],
        compiler_params=pltpu.CompilerParams(vmem_limit_bytes=VMEM_LIMIT),
        cost_estimate=pl.CostEstimate(
            flops=2 * 2 * rows * 2 * depth * 4 * cols, bytes_accessed=12 << 20, transcendentals=0
        ),
    )(place, *attn, *weights)


def after(array, *earlier):
    return lax.optimization_barrier((array,) + earlier)[0]


def split_body(tokens, w_query, key_matrix, value_matrix, w_out):
    ctx, x = lax.axis_index("ctx"), lax.axis_index("fsdp")
    place = jnp.stack([ctx, x]).astype(jnp.int32)
    z = ctx // 4
    rows = tokens.shape[0]
    group = w_query.shape[1] // 4

    def columns(weight, head, width):
        return lax.dynamic_slice_in_dim(weight, head * width, width, 1)

    def pair(head):
        parts = [columns(w, head, HEAD_SIZE) for w in (key_matrix, value_matrix)]
        return jnp.concatenate(parts, axis=1)

    wide = 2 * HEAD_SIZE

    tok1 = across_z(tokens, 1)
    tok2 = across_z(tokens, 2)
    other0 = across_x(tokens)
    x_out = across_x(w_out)
    own = jnp.concatenate([pair(z), columns(w_query, z, group)], axis=1)
    own_y = across_y(own)
    y_out = across_y(after(w_out, own_y))
    far_half = [columns(w, 1 - z // 2, wide) for w in (key_matrix, value_matrix)]
    far = across_z(after(jnp.concatenate(far_half, axis=1), tok1, other0, own_y), 2)

    def far_pair(head):
        parts = [columns(w, head, HEAD_SIZE) for w in (far[:, :wide], far[:, wide:])]
        return jnp.concatenate(parts, axis=1)

    other1 = across_x(after(tok1, other0, own_y))
    tok3 = across_z(after(tok2, tok1, x_out, own_y), 1)
    xy_out = across_y(after(x_out, own_y))
    other2 = across_x(after(tok2, other1))
    near = across_z(after(jnp.stack([pair(z ^ 1), far_pair(1 - z % 2)]), y_out), 1)
    query2 = across_z(after(columns(w_query, z ^ 2, group), far), 2)
    query3 = across_z(after(columns(w_query, z ^ 3, group), far, tok3, other1), 3)
    other3 = across_x(after(tok3, other1))
    query1 = across_z(after(columns(w_query, z ^ 1, group), far, near), 1)
    token_pieces = [tokens, other0, tok1, other1, tok2, other2, tok3, other3]

    both = jnp.stack([own, own_y])
    both_core = across_core(after(both, other1))
    kv_rest = jnp.stack([near[0], far_pair(z % 2), near[1]])
    kv_rest_y = across_y(after(kv_rest, both_core, y_out, xy_out, other2))
    query2_y = across_y(after(query2, kv_rest_y))
    query31_y = across_y(after(jnp.stack([query3, query1]), kv_rest_y))
    kv_core = across_core(after(jnp.concatenate([kv_rest, kv_rest_y]), other3))
    kv_weights = [both, both_core, kv_rest, kv_rest_y, kv_core]
    kv_plan = ((0, 2), (1, 3), (4, 8, 12), (6, 10, 14), (5, 9, 13, 7, 11, 15))

    slot = jnp.arange(4, dtype=jnp.int32)[:, None]
    positions = (ctx ^ (4 * slot)) * rows + jnp.arange(rows, dtype=jnp.int32)[None, :]
    cosine, sine = rotary_tables(positions.reshape(-1))
    cosine = jnp.concatenate([cosine, cosine], axis=1)
    sine = jnp.concatenate([-sine, sine], axis=1)

    own_kv = project(
        kv_kernel,
        (4, rows, wide),
        place,
        token_pieces,
        kv_weights,
        kv_plan,
        wide,
        cosine,
        sine,
    )
    y_kv = across_y(own_kv)
    kv = [own_kv, across_core(own_kv), y_kv, across_core(y_kv)]
    query_rest = jnp.stack([query1, query2, query3, query31_y[1], query2_y, query31_y[0]])
    query_core = across_core(after(query_rest, own_kv))
    query_weights = [both, both_core, query_rest, query_core]
    query_plan = ((0, 2), (1, 3), (4, 8, 12, 6, 10, 14), (5, 9, 13, 7, 11, 15))
    queries = project(
        query_kernel,
        (4, group // HEAD_SIZE * rows, HEAD_SIZE),
        place,
        token_pieces,
        query_weights,
        query_plan,
        group,
        cosine,
        sine,
    )
    mine, other = attend(place, queries, kv)
    out_weights = []
    for piece in (w_out, x_out, y_out, xy_out):
        out_weights += [piece, across_core(piece)]
    mine, other = after(mine, *out_weights), after(other, *out_weights)
    mine2 = across_z(mine, 2)
    mine1 = across_z(mine, 1)
    from_x = across_x(other)
    from_x2 = across_z(from_x, 2)
    from_x1 = across_z(after(from_x, mine1), 1)
    mine3 = across_z(mine2, 1)
    from_x3 = across_z(from_x2, 1)
    attn = [mine, mine1, mine2, mine3, from_x, from_x1, from_x2, from_x3]

    first, second = project_out(place, attn, out_weights)

    def home(m):
        return lambda z, y, c, x: (x ^ 3 * (z % 2 ^ m), y, c, z // 2)

    first, second = move(first, home(0)), move(second, home(1))
    odd = z // 2 == 1
    return jnp.concatenate(
        [jnp.where(odd, second, first), jnp.where(odd, first, second)], axis=1
    )


def solution(mesh):
    in_specs = (
        P("ctx", "fsdp"),
        P("ctx", "fsdp"),
        P("ctx", "fsdp"),
        P("ctx", "fsdp"),
        P("fsdp", "ctx"),
    )
    out_specs = P("ctx", "fsdp")
    split = mesh.shape["ctx"] == 16 and mesh.shape["fsdp"] == 2
    body = split_body if split else gathered_body
    return jax.shard_map(body, mesh=mesh, in_specs=in_specs, out_specs=out_specs, check_vma=False)
```

```python
import functools
import math

import jax
import jax.numpy as jnp
from jax import lax
from jax.experimental import pallas as pl
from jax.experimental.pallas import tpu as pltpu
from jax.sharding import PartitionSpec as P

HEAD_SIZE = 128
AXES = ("ctx", "fsdp")
VMEM_LIMIT = 18 * 1024 * 1024


def rotary_tables(positions):
    half_dim = HEAD_SIZE // 2
    inverse_freq = jnp.power(
        jnp.float32(500000.0), -jnp.arange(half_dim, dtype=jnp.float32) * 2.0 / HEAD_SIZE
    )
    angles = positions.astype(jnp.float32)[:, None] * inverse_freq[None, :]
    return jnp.cos(angles), jnp.sin(angles)


def rotate_heads(values, positions):
    tok_count = values.shape[0]
    head_count = values.shape[1] // HEAD_SIZE
    half_dim = HEAD_SIZE // 2
    cosine, sine_table = rotary_tables(positions)
    cosine, sine_table = cosine[:, None, :], sine_table[:, None, :]
    shaped = values.reshape(tok_count, head_count, HEAD_SIZE)
    first_half = shaped[:, :, :half_dim]
    second = shaped[:, :, half_dim:]
    turned = jnp.concatenate(
        [first_half * cosine - second * sine_table, second * cosine + first_half * sine_table],
        axis=2,
    )
    return turned.reshape(tok_count, head_count * HEAD_SIZE).astype(jnp.bfloat16)


def gathered_body(tokens, w_query, key_matrix, value_matrix, w_out):
    features = lax.all_gather(tokens, "fsdp", axis=1, tiled=True)
    tok_count = features.shape[0]
    positions = lax.axis_index("ctx") * tok_count + jnp.arange(tok_count, dtype=jnp.int32)

    def add_rows(weight_piece):
        return jnp.dot(features, weight_piece, preferred_element_type=jnp.float32)

    query_sum = add_rows(lax.all_gather(w_query, "ctx", axis=0, tiled=True))
    key_sum = add_rows(lax.all_gather(key_matrix, "ctx", axis=0, tiled=True))
    value_sum = add_rows(lax.all_gather(value_matrix, "ctx", axis=0, tiled=True))
    queries = rotate_heads(query_sum, positions)
    projected_keys = rotate_heads(key_sum, positions)
    projected_values = value_sum.astype(jnp.bfloat16)
    kv_heads = projected_keys.shape[1] // HEAD_SIZE
    queries_per_group = queries.shape[1] // projected_keys.shape[1]
    stacked = (
        queries.reshape(tok_count, kv_heads, queries_per_group, HEAD_SIZE)
        .transpose(1, 2, 0, 3)
        .reshape(kv_heads, queries_per_group * tok_count, HEAD_SIZE)
    )
    query_pos = jnp.tile(positions, queries_per_group)
    score_scale = 1.0 / math.sqrt(HEAD_SIZE)

    def update(attn_state, key_block, value_block, key_start):
        row_max, row_total, accum = attn_state
        block_rows = key_block.shape[0]
        key_heads = key_block.reshape(block_rows, kv_heads, HEAD_SIZE)
        value_heads = value_block.reshape(block_rows, kv_heads, HEAD_SIZE)
        scores = (
            jnp.einsum("gqd,kgd->gqk", stacked, key_heads, preferred_element_type=jnp.float32)
            * score_scale
        )
        key_pos = key_start + jnp.arange(block_rows, dtype=jnp.int32)
        allowed = (key_pos[None, :] <= query_pos[:, None])[None]
        masked = jnp.where(allowed, scores, jnp.float32(-1e30))
        new_max = jnp.maximum(row_max, jnp.max(masked, axis=2))
        exp_weights = jnp.where(allowed, jnp.exp(masked - new_max[:, :, None]), jnp.float32(0.0))
        factor = jnp.exp(row_max - new_max)
        row_total = row_total * factor + jnp.sum(exp_weights, axis=2)
        accum = accum * factor[:, :, None] + jnp.einsum(
            "gqk,kgd->gqd",
            exp_weights.astype(jnp.bfloat16),
            value_heads,
            preferred_element_type=jnp.float32,
        )
        return (new_max, row_total, accum)

    query_rows = queries_per_group * tok_count
    initial = (
        jnp.full((kv_heads, query_rows), -1e30, jnp.float32),
        jnp.zeros((kv_heads, query_rows), jnp.float32),
        jnp.zeros((kv_heads, query_rows, HEAD_SIZE), jnp.float32),
    )
    key_piece = lax.all_gather(projected_keys, "ctx", axis=0, tiled=True)
    value_piece = lax.all_gather(projected_values, "ctx", axis=0, tiled=True)
    block_rows = min(tok_count, key_piece.shape[0])
    block_count = key_piece.shape[0] // block_rows

    def advance(block_index, carried):
        key_start = block_index * block_rows
        key_block = lax.dynamic_slice_in_dim(key_piece, block_index * block_rows, block_rows, 0)
        value_block = lax.dynamic_slice_in_dim(value_piece, block_index * block_rows, block_rows, 0)
        return update(carried, key_block, value_block, key_start)

    row_max, row_total, accum = lax.fori_loop(0, block_count, advance, initial)
    normed = accum / row_total[:, :, None]
    attn_out = (
        normed.reshape(kv_heads, queries_per_group, tok_count, HEAD_SIZE)
        .transpose(2, 0, 1, 3)
        .reshape(tok_count, kv_heads * queries_per_group * HEAD_SIZE)
        .astype(jnp.bfloat16)
    )
    partial_out = jnp.dot(
        attn_out,
        lax.all_gather(w_out, "ctx", axis=1, tiled=True),
        preferred_element_type=jnp.float32,
    )
    return lax.psum_scatter(
        partial_out.astype(jnp.bfloat16), "fsdp", scatter_dimension=1, tiled=True
    )


def moves(target):
    pairs = []
    for i in range(32):
        z, y, c, x = i // 8, i // 4 % 2, i // 2 % 2, i % 2
        tz, ty, tc, tx = target(z, y, c, x)
        pairs.append((i, tz * 8 + ty * 4 + tc * 2 + tx))
    return pairs


def any_specs(count):
    return [pl.BlockSpec(memory_space=pl.ANY)] * count


def smem_spec():
    return pl.BlockSpec(memory_space=pltpu.SMEM)


def vmem_spec():
    return pl.BlockSpec(memory_space=pltpu.VMEM)


def load_projection(place, token_refs, weight_refs, plan, first_column, tok, wgt, sems):
    ctx, x = place[0], place[1]
    rows, half = token_refs[0].shape
    depth, width = wgt.shape[0] // 16, wgt.shape[1]
    copies = []
    for m in range(4):
        for rx in range(2):
            into = tok.at[pl.ds(m * rows, rows), pl.ds(pl.multiple_of((x ^ rx) * half, half), half)]
            copies.append((token_refs[m * 2 + rx], into))
    for ref, blocks in zip(weight_refs, plan, strict=True):
        at = first_column if ref.shape[-1] > width else 0
        for k, relative in enumerate(blocks):
            into = wgt.at[pl.ds(pl.multiple_of((ctx ^ relative) * depth, depth), depth)]
            copies.append((ref.at[k, :, pl.ds(at, width)], into))
    handles = [pltpu.make_async_copy(s, d, sems.at[i]) for i, (s, d) in enumerate(copies)]
    for handle in handles:
        handle.start()
    for handle in handles:
        handle.wait()


def rotated(values, cosine, sine):
    turned = jnp.concatenate([values[:, HEAD_SIZE // 2 :], values[:, : HEAD_SIZE // 2]], axis=1)
    return values * cosine + turned * sine


def kv_kernel(plan, place, *refs):
    token_refs, weight_refs = refs[:8], refs[8:-6]
    cosine, sine, out, tok, wgt, sems = refs[-6:]
    load_projection(place, token_refs, weight_refs, plan, 0, tok, wgt, sems)
    rows = tok.shape[0] // 4
    values = jnp.dot(tok[...], wgt[...], preferred_element_type=jnp.float32)
    keys = rotated(values[:, :HEAD_SIZE], cosine[...], sine[...]).astype(jnp.bfloat16)
    vals = values[:, HEAD_SIZE:].astype(jnp.bfloat16)
    for m in range(4):
        out[m, :, :HEAD_SIZE] = keys[m * rows : (m + 1) * rows]
        out[m, :, HEAD_SIZE:] = vals[m * rows : (m + 1) * rows]


def query_kernel(plan, place, *refs):
    token_refs, weight_refs = refs[:8], refs[8:-6]
    cosine, sine, out, tok, wgt, sems = refs[-6:]
    load_projection(place, token_refs, weight_refs, plan, 2 * HEAD_SIZE, tok, wgt, sems)
    rows = tok.shape[0] // 4
    heads = wgt.shape[1] // HEAD_SIZE
    for pair in range(heads // 2):
        values = jnp.dot(
            tok[...],
            wgt[:, pair * 2 * HEAD_SIZE : (pair + 1) * 2 * HEAD_SIZE],
            preferred_element_type=jnp.float32,
        )
        for k in range(2):
            one = rotated(values[:, k * HEAD_SIZE : (k + 1) * HEAD_SIZE], cosine[...], sine[...])
            one = one.astype(jnp.bfloat16)
            head = pair * 2 + k
            for m in range(4):
                out[m, head * rows : (head + 1) * rows, :] = one[m * rows : (m + 1) * rows]


def project(kernel, out_shape, place, tokens, weights, plan, width, cosine, sine):
    rows, half = tokens[0].shape
    depth = weights[0].shape[1]
    flops = 16 * 4 * rows * 16 * depth * HEAD_SIZE * 4
    return pl.pallas_call(
        functools.partial(kernel, plan),
        out_shape=jax.ShapeDtypeStruct(out_shape, jnp.bfloat16),
        in_specs=[smem_spec()] + any_specs(8 + len(weights)) + [vmem_spec()] * 2,
        out_specs=vmem_spec(),
        scratch_shapes=[
            pltpu.VMEM((4 * rows, 2 * half), jnp.bfloat16),
            pltpu.VMEM((16 * depth, width), jnp.bfloat16),
            pltpu.SemaphoreType.DMA((24,)),
        ],
        compiler_params=pltpu.CompilerParams(vmem_limit_bytes=VMEM_LIMIT),
        cost_estimate=pl.CostEstimate(flops=flops, bytes_accessed=8 << 20, transcendentals=0),
    )(place, *tokens, *weights, cosine, sine)


def attend_kernel(place, queries, kv0, kv1, kv2, kv3, mine, other, store, sems):
    ctx, x = place[0], place[1]
    rows = kv0.shape[1]
    handles = []
    for r, ref in enumerate((kv0, kv1, kv2, kv3)):
        for m in range(4):
            block = ctx ^ (4 * m + r)
            into = store.at[pl.ds(pl.multiple_of(block * rows, rows), rows)]
            handles.append(pltpu.make_async_copy(ref.at[m], into, sems.at[4 * r + m]))
    for handle in handles:
        handle.start()
    for handle in handles:
        handle.wait()
    z, e = ctx // 4, ctx % 4
    scale = math.log2(math.e) / math.sqrt(HEAD_SIZE)
    span = 4 * rows
    heads = queries.shape[1] // rows
    group = 2
    row = lax.broadcasted_iota(jnp.int32, (group * rows, span), 0) % rows + e * rows
    column = lax.broadcasted_iota(jnp.int32, (group * rows, span), 1)
    allowed = column <= row

    def block_of(block, out):
        count = (block + 1) * span
        keys, values = store[:count, :HEAD_SIZE], store[:count, HEAD_SIZE:]
        for first in range(0, heads, group):
            query = queries[z ^ block, pl.ds(first * rows, group * rows), :]
            scores = lax.dot_general(
                query, keys, (((1,), (1,)), ((), ())), preferred_element_type=jnp.float32
            )
            last = jnp.where(allowed, scores[:, count - span :], jnp.float32(-1e30))
            scores = jnp.concatenate([scores[:, : count - span], last], axis=1) if block else last
            top = jnp.max(scores, axis=1, keepdims=True)
            weights = jnp.exp2((scores - top) * jnp.float32(scale))
            total = jnp.sum(weights, axis=1, keepdims=True)
            summed = jnp.dot(
                weights.astype(jnp.bfloat16), values, preferred_element_type=jnp.float32
            )
            normed = (summed / total).astype(jnp.bfloat16)
            for k in range(group):
                at = slice((first + k) * HEAD_SIZE, (first + k + 1) * HEAD_SIZE)
                out[block // 2, :, at] = normed[k * rows : (k + 1) * rows]

    @pl.when(x == 0)
    def _():
        for block in range(4):
            block_of(block, mine if block in (0, 3) else other)

    @pl.when(x == 1)
    def _():
        for block in range(4):
            block_of(block, mine if block in (1, 2) else other)


def attend(place, queries, kv):
    _, stacked, _ = queries.shape
    rows = kv[0].shape[1]
    heads = stacked // rows
    shape = jax.ShapeDtypeStruct((2, rows, heads * HEAD_SIZE), jnp.bfloat16)
    work = 4 * stacked * 16 * rows * HEAD_SIZE
    return pl.pallas_call(
        attend_kernel,
        out_shape=(shape, shape),
        in_specs=[smem_spec(), vmem_spec()] + any_specs(4),
        out_specs=(vmem_spec(), vmem_spec()),
        scratch_shapes=[
            pltpu.VMEM((16 * rows, 2 * HEAD_SIZE), jnp.bfloat16),
            pltpu.SemaphoreType.DMA((16,)),
        ],
        compiler_params=pltpu.CompilerParams(vmem_limit_bytes=VMEM_LIMIT),
        cost_estimate=pl.CostEstimate(
            flops=20 * work, bytes_accessed=4 << 20, transcendentals=4 * stacked * 16 * rows
        ),
    )(place, queries, *kv)


def output_kernel(place, *refs):
    attn_refs, weight_refs = refs[:8], refs[8:16]
    out0, out1, attn, wgt, sems = refs[16:]
    ctx, x = place[0], place[1]
    z, y, c = ctx // 4, ctx // 2 % 2, ctx % 2
    _, rows, width = attn_refs[0].shape
    depth, cols = weight_refs[0].shape
    handles = []
    for rx in range(2):
        for m in range(4):
            at = (x ^ rx) * depth + (z ^ m) * width
            into = attn.at[:, :, pl.ds(pl.multiple_of(at, width), width)]
            n = rx * 4 + m
            handles.append(pltpu.make_async_copy(attn_refs[n], into, sems.at[n]))
    for n in range(8):
        ry, rx, rc = n // 4, n // 2 % 2, n % 2
        at = ((y ^ ry) * 2 + (c ^ rc)) * cols
        into = wgt.at[
            pl.ds(pl.multiple_of((x ^ rx) * depth, depth), depth),
            pl.ds(pl.multiple_of(at, cols), cols),
        ]
        handles.append(pltpu.make_async_copy(weight_refs[n], into, sems.at[8 + n]))
    for handle in handles:
        handle.start()
    for handle in handles:
        handle.wait()
    low = z % 2
    for part in range(4):
        at = slice(part * cols, (part + 1) * cols)
        terms = []
        for f in range(2):
            term = jnp.dot(
                attn[:, :, f * depth : (f + 1) * depth].reshape(2 * rows, depth),
                wgt[f * depth : (f + 1) * depth, at],
                preferred_element_type=jnp.float32,
            )
            terms.append(term.astype(jnp.bfloat16).astype(jnp.float32))
        mixed = (terms[0] + terms[1]).astype(jnp.bfloat16)
        first, second = mixed[:rows], mixed[rows:]

        @pl.when(low == 0)
        def _():
            out0[:, at] = first
            out1[:, at] = second

        @pl.when(low == 1)
        def _():
            out0[:, at] = second
            out1[:, at] = first


def project_out(place, attn, weights):
    _, rows, width = attn[0].shape
    depth, cols = weights[0].shape
    shape = jax.ShapeDtypeStruct((rows, 4 * cols), jnp.bfloat16)
    return pl.pallas_call(
        output_kernel,
        out_shape=(shape, shape),
        in_specs=[smem_spec()] + any_specs(16),
        out_specs=(vmem_spec(), vmem_spec()),
        scratch_shapes=[
            pltpu.VMEM((2, rows, 2 * depth), jnp.bfloat16),
            pltpu.VMEM((2 * depth, 4 * cols), jnp.bfloat16),
            pltpu.SemaphoreType.DMA((16,)),
        ],
        compiler_params=pltpu.CompilerParams(vmem_limit_bytes=VMEM_LIMIT),
        cost_estimate=pl.CostEstimate(
            flops=2 * 2 * rows * 2 * depth * 4 * cols, bytes_accessed=12 << 20, transcendentals=0
        ),
    )(place, *attn, *weights)


ORDER = {
    "y_out": ("own_y",),
    "far": ("tok1", "other0", "own_y"),
    "other1": ("other0", "own_y"),
    "tok3": ("tok2", "tok1", "x_out", "own_y"),
    "xy_out": ("own_y",),
    "other2": ("other1",),
    "near": ("y_out",),
    "query2": ("far",),
    "query3": ("far", "tok3", "other1"),
    "other3": ("other1",),
    "query1": ("far", "near"),
    "both_core": ("other1",),
    "kv_rest_y": ("both_core", "y_out", "xy_out", "other2"),
    "query2_y": ("kv_rest_y",),
    "query31_y": ("kv_rest_y",),
    "kv_core": ("other3",),
    "query_core": ("own_kv",),
    "mine1": ("core_w", "core_x", "core_y", "core_xy"),
    "mine2": ("core_w", "core_x", "core_y", "core_xy"),
    "from_x": ("core_w", "core_x", "core_y", "core_xy"),
    "from_x1": ("mine1",),
    "core_y_kv": ("queries",),
}


class Transfers:
    def __init__(self):
        self.there = {}

    def __call__(self, name, array, target):
        earlier = [self.there[k] for k in ORDER.get(name, ())]
        if earlier:
            array = lax.optimization_barrier((array, *earlier))[0]
        self.there[name] = lax.ppermute(array, AXES, moves(target))
        return self.there[name]


def to_z(m):
    return lambda z, y, c, x: (z ^ m, y, c, x)


def to_y(z, y, c, x):
    return (z, 1 - y, c, x)


def to_core(z, y, c, x):
    return (z, y, 1 - c, x)


def to_x(z, y, c, x):
    return (z, y, c, 1 - x)


def split_body(tokens, w_query, key_matrix, value_matrix, w_out):
    ctx, x = lax.axis_index("ctx"), lax.axis_index("fsdp")
    place = jnp.stack([ctx, x]).astype(jnp.int32)
    z = ctx // 4
    rows = tokens.shape[0]
    group, wide = w_query.shape[1] // 4, 2 * HEAD_SIZE
    send = Transfers()

    def columns(weight, head, width):
        return lax.dynamic_slice_in_dim(weight, head * width, width, 1)

    def pair(head):
        parts = [columns(w, head, HEAD_SIZE) for w in (key_matrix, value_matrix)]
        return jnp.concatenate(parts, axis=1)

    tok1 = send("tok1", tokens, to_z(1))
    tok2 = send("tok2", tokens, to_z(2))
    other0 = send("other0", tokens, to_x)
    x_out = send("x_out", w_out, to_x)
    own = jnp.concatenate([pair(z), columns(w_query, z, group)], axis=1)
    own_y = send("own_y", own, to_y)
    y_out = send("y_out", w_out, to_y)
    far_half = [columns(w, 1 - z // 2, wide) for w in (key_matrix, value_matrix)]
    far = send("far", jnp.concatenate(far_half, axis=1), to_z(2))

    def far_pair(head):
        parts = [columns(w, head, HEAD_SIZE) for w in (far[:, :wide], far[:, wide:])]
        return jnp.concatenate(parts, axis=1)

    other1 = send("other1", tok1, to_x)
    tok3 = send("tok3", tok2, to_z(1))
    xy_out = send("xy_out", x_out, to_y)
    other2 = send("other2", tok2, to_x)
    near = send("near", jnp.stack([pair(z ^ 1), far_pair(1 - z % 2)]), to_z(1))
    query2 = send("query2", columns(w_query, z ^ 2, group), to_z(2))
    query3 = send("query3", columns(w_query, z ^ 3, group), to_z(3))
    other3 = send("other3", tok3, to_x)
    query1 = send("query1", columns(w_query, z ^ 1, group), to_z(1))
    token_pieces = [tokens, other0, tok1, other1, tok2, other2, tok3, other3]

    both = jnp.stack([own, own_y])
    both_core = send("both_core", both, to_core)
    kv_rest = jnp.stack([near[0], far_pair(z % 2), near[1]])
    kv_rest_y = send("kv_rest_y", kv_rest, to_y)
    query2_y = send("query2_y", query2, to_y)
    query31_y = send("query31_y", jnp.stack([query3, query1]), to_y)
    kv_core = send("kv_core", jnp.concatenate([kv_rest, kv_rest_y]), to_core)
    kv_weights = [both, both_core, kv_rest, kv_rest_y, kv_core]
    kv_plan = ((0, 2), (1, 3), (4, 8, 12), (6, 10, 14), (5, 9, 13, 7, 11, 15))

    slot = jnp.arange(4, dtype=jnp.int32)[:, None]
    positions = (ctx ^ (4 * slot)) * rows + jnp.arange(rows, dtype=jnp.int32)[None, :]
    cosine, sine = rotary_tables(positions.reshape(-1))
    cosine = jnp.concatenate([cosine, cosine], axis=1)
    sine = jnp.concatenate([-sine, sine], axis=1)

    own_kv = project(
        kv_kernel,
        (4, rows, wide),
        place,
        token_pieces,
        kv_weights,
        kv_plan,
        wide,
        cosine,
        sine,
    )
    send.there["own_kv"] = own_kv
    y_kv = send("y_kv", own_kv, to_y)
    core_kv = send("core_kv", own_kv, to_core)
    query_rest = jnp.stack([query1, query2, query3, query31_y[1], query2_y, query31_y[0]])
    query_core = send("query_core", query_rest, to_core)
    query_weights = [both, both_core, query_rest, query_core]
    query_plan = ((0, 2), (1, 3), (4, 8, 12, 6, 10, 14), (5, 9, 13, 7, 11, 15))
    queries = project(
        query_kernel,
        (4, group // HEAD_SIZE * rows, HEAD_SIZE),
        place,
        token_pieces,
        query_weights,
        query_plan,
        group,
        cosine,
        sine,
    )
    send.there["queries"] = queries
    core_y_kv = send("core_y_kv", y_kv, to_core)
    kv = [own_kv, core_kv, y_kv, core_y_kv]
    mine, other = attend(place, queries, kv)
    send.there["attend"] = mine
    out_weights = []
    for name, piece in (("w", w_out), ("x", x_out), ("y", y_out), ("xy", xy_out)):
        out_weights += [piece, send("core_" + name, piece, to_core)]
    mine2 = send("mine2", mine, to_z(2))
    mine1 = send("mine1", mine, to_z(1))
    from_x = send("from_x", other, to_x)
    from_x2 = send("from_x2", from_x, to_z(2))
    from_x1 = send("from_x1", from_x, to_z(1))
    mine3 = send("mine3", mine2, to_z(1))
    from_x3 = send("from_x3", from_x2, to_z(1))
    attn = [mine, mine1, mine2, mine3, from_x, from_x1, from_x2, from_x3]

    first, second = project_out(place, attn, out_weights)

    def home(m):
        return lambda z, y, c, x: (x ^ 3 * (z % 2 ^ m), y, c, z // 2)

    first, second = send("home0", first, home(0)), send("home1", second, home(1))
    odd = z // 2 == 1
    return jnp.concatenate(
        [jnp.where(odd, second, first), jnp.where(odd, first, second)], axis=1
    )


def solution(mesh):
    in_specs = (
        P("ctx", "fsdp"),
        P("ctx", "fsdp"),
        P("ctx", "fsdp"),
        P("ctx", "fsdp"),
        P("fsdp", "ctx"),
    )
    out_specs = P("ctx", "fsdp")
    split = mesh.shape["ctx"] == 16 and mesh.shape["fsdp"] == 2
    body = split_body if split else gathered_body
    return jax.shard_map(body, mesh=mesh, in_specs=in_specs, out_specs=out_specs, check_vma=False)
```

```python
import functools
import math

import jax
import jax.numpy as jnp
from jax import lax
from jax.experimental import pallas as pl
from jax.experimental.pallas import tpu as pltpu
from jax.sharding import PartitionSpec as P

HEAD_SIZE = 128
AXES = ("ctx", "fsdp")
VMEM_LIMIT = 18 * 1024 * 1024


def rotary_tables(positions):
    half_dim = HEAD_SIZE // 2
    inverse_freq = jnp.power(
        jnp.float32(500000.0), -jnp.arange(half_dim, dtype=jnp.float32) * 2.0 / HEAD_SIZE
    )
    angles = positions.astype(jnp.float32)[:, None] * inverse_freq[None, :]
    return jnp.cos(angles), jnp.sin(angles)


def rotate_heads(values, positions):
    tok_count = values.shape[0]
    head_count = values.shape[1] // HEAD_SIZE
    half_dim = HEAD_SIZE // 2
    cosine, sine_table = rotary_tables(positions)
    cosine, sine_table = cosine[:, None, :], sine_table[:, None, :]
    shaped = values.reshape(tok_count, head_count, HEAD_SIZE)
    first_half = shaped[:, :, :half_dim]
    second = shaped[:, :, half_dim:]
    turned = jnp.concatenate(
        [first_half * cosine - second * sine_table, second * cosine + first_half * sine_table],
        axis=2,
    )
    return turned.reshape(tok_count, head_count * HEAD_SIZE).astype(jnp.bfloat16)


def gathered_body(tokens, w_query, key_matrix, value_matrix, w_out):
    features = lax.all_gather(tokens, "fsdp", axis=1, tiled=True)
    tok_count = features.shape[0]
    positions = lax.axis_index("ctx") * tok_count + jnp.arange(tok_count, dtype=jnp.int32)

    def add_rows(weight_piece):
        return jnp.dot(features, weight_piece, preferred_element_type=jnp.float32)

    query_sum = add_rows(lax.all_gather(w_query, "ctx", axis=0, tiled=True))
    key_sum = add_rows(lax.all_gather(key_matrix, "ctx", axis=0, tiled=True))
    value_sum = add_rows(lax.all_gather(value_matrix, "ctx", axis=0, tiled=True))
    queries = rotate_heads(query_sum, positions)
    projected_keys = rotate_heads(key_sum, positions)
    projected_values = value_sum.astype(jnp.bfloat16)
    kv_heads = projected_keys.shape[1] // HEAD_SIZE
    queries_per_group = queries.shape[1] // projected_keys.shape[1]
    stacked = (
        queries.reshape(tok_count, kv_heads, queries_per_group, HEAD_SIZE)
        .transpose(1, 2, 0, 3)
        .reshape(kv_heads, queries_per_group * tok_count, HEAD_SIZE)
    )
    query_pos = jnp.tile(positions, queries_per_group)
    score_scale = 1.0 / math.sqrt(HEAD_SIZE)

    def update(attn_state, key_block, value_block, key_start):
        row_max, row_total, accum = attn_state
        block_rows = key_block.shape[0]
        key_heads = key_block.reshape(block_rows, kv_heads, HEAD_SIZE)
        value_heads = value_block.reshape(block_rows, kv_heads, HEAD_SIZE)
        scores = (
            jnp.einsum("gqd,kgd->gqk", stacked, key_heads, preferred_element_type=jnp.float32)
            * score_scale
        )
        key_pos = key_start + jnp.arange(block_rows, dtype=jnp.int32)
        allowed = (key_pos[None, :] <= query_pos[:, None])[None]
        masked = jnp.where(allowed, scores, jnp.float32(-1e30))
        new_max = jnp.maximum(row_max, jnp.max(masked, axis=2))
        exp_weights = jnp.where(allowed, jnp.exp(masked - new_max[:, :, None]), jnp.float32(0.0))
        factor = jnp.exp(row_max - new_max)
        row_total = row_total * factor + jnp.sum(exp_weights, axis=2)
        accum = accum * factor[:, :, None] + jnp.einsum(
            "gqk,kgd->gqd",
            exp_weights.astype(jnp.bfloat16),
            value_heads,
            preferred_element_type=jnp.float32,
        )
        return (new_max, row_total, accum)

    query_rows = queries_per_group * tok_count
    initial = (
        jnp.full((kv_heads, query_rows), -1e30, jnp.float32),
        jnp.zeros((kv_heads, query_rows), jnp.float32),
        jnp.zeros((kv_heads, query_rows, HEAD_SIZE), jnp.float32),
    )
    key_piece = lax.all_gather(projected_keys, "ctx", axis=0, tiled=True)
    value_piece = lax.all_gather(projected_values, "ctx", axis=0, tiled=True)
    block_rows = min(tok_count, key_piece.shape[0])
    block_count = key_piece.shape[0] // block_rows

    def advance(block_index, carried):
        key_start = block_index * block_rows
        key_block = lax.dynamic_slice_in_dim(key_piece, block_index * block_rows, block_rows, 0)
        value_block = lax.dynamic_slice_in_dim(value_piece, block_index * block_rows, block_rows, 0)
        return update(carried, key_block, value_block, key_start)

    row_max, row_total, accum = lax.fori_loop(0, block_count, advance, initial)
    normed = accum / row_total[:, :, None]
    attn_out = (
        normed.reshape(kv_heads, queries_per_group, tok_count, HEAD_SIZE)
        .transpose(2, 0, 1, 3)
        .reshape(tok_count, kv_heads * queries_per_group * HEAD_SIZE)
        .astype(jnp.bfloat16)
    )
    partial_out = jnp.dot(
        attn_out,
        lax.all_gather(w_out, "ctx", axis=1, tiled=True),
        preferred_element_type=jnp.float32,
    )
    return lax.psum_scatter(
        partial_out.astype(jnp.bfloat16), "fsdp", scatter_dimension=1, tiled=True
    )


def moves(target):
    pairs = []
    for i in range(32):
        z, y, c, x = i // 8, i // 4 % 2, i // 2 % 2, i % 2
        tz, ty, tc, tx = target(z, y, c, x)
        pairs.append((i, tz * 8 + ty * 4 + tc * 2 + tx))
    return pairs


def any_specs(count):
    return [pl.BlockSpec(memory_space=pl.ANY)] * count


def smem_spec():
    return pl.BlockSpec(memory_space=pltpu.SMEM)


def vmem_spec():
    return pl.BlockSpec(memory_space=pltpu.VMEM)


def load_projection(place, token_refs, weight_refs, plan, first_column, tok, wgt, sems):
    ctx, x = place[0], place[1]
    rows, half = token_refs[0].shape
    depth, width = wgt.shape[0] // 16, wgt.shape[1]
    copies = []
    for m in range(4):
        for rx in range(2):
            into = tok.at[pl.ds(m * rows, rows), pl.ds(pl.multiple_of((x ^ rx) * half, half), half)]
            copies.append((token_refs[m * 2 + rx], into))
    for ref, blocks in zip(weight_refs, plan, strict=True):
        at = first_column if ref.shape[-1] > width else 0
        for k, relative in enumerate(blocks):
            into = wgt.at[pl.ds(pl.multiple_of((ctx ^ relative) * depth, depth), depth)]
            copies.append((ref.at[k, :, pl.ds(at, width)], into))
    handles = [pltpu.make_async_copy(s, d, sems.at[i]) for i, (s, d) in enumerate(copies)]
    for handle in handles:
        handle.start()
    for handle in handles:
        handle.wait()


def rotated(values, cosine, sine):
    turned = jnp.concatenate([values[:, HEAD_SIZE // 2 :], values[:, : HEAD_SIZE // 2]], axis=1)
    return values * cosine + turned * sine


def kv_kernel(plan, place, *refs):
    token_refs, weight_refs = refs[:8], refs[8:-6]
    cosine, sine, out, tok, wgt, sems = refs[-6:]
    load_projection(place, token_refs, weight_refs, plan, 0, tok, wgt, sems)
    rows = tok.shape[0] // 4
    values = jnp.dot(tok[...], wgt[...], preferred_element_type=jnp.float32)
    keys = rotated(values[:, :HEAD_SIZE], cosine[...], sine[...]).astype(jnp.bfloat16)
    vals = values[:, HEAD_SIZE:].astype(jnp.bfloat16)
    for m in range(4):
        out[m, :, :HEAD_SIZE] = keys[m * rows : (m + 1) * rows]
        out[m, :, HEAD_SIZE:] = vals[m * rows : (m + 1) * rows]


def query_kernel(plan, place, *refs):
    token_refs, weight_refs = refs[:8], refs[8:-6]
    cosine, sine, out, tok, wgt, sems = refs[-6:]
    load_projection(place, token_refs, weight_refs, plan, 2 * HEAD_SIZE, tok, wgt, sems)
    rows = tok.shape[0] // 4
    heads = wgt.shape[1] // HEAD_SIZE
    for pair in range(heads // 2):
        values = jnp.dot(
            tok[...],
            wgt[:, pair * 2 * HEAD_SIZE : (pair + 1) * 2 * HEAD_SIZE],
            preferred_element_type=jnp.float32,
        )
        for k in range(2):
            one = rotated(values[:, k * HEAD_SIZE : (k + 1) * HEAD_SIZE], cosine[...], sine[...])
            one = one.astype(jnp.bfloat16)
            head = pair * 2 + k
            for m in range(4):
                out[m, head * rows : (head + 1) * rows, :] = one[m * rows : (m + 1) * rows]


def project(kernel, out_shape, place, tokens, weights, plan, width, cosine, sine):
    rows, half = tokens[0].shape
    depth = weights[0].shape[1]
    flops = 1 * 4 * rows * 16 * depth * HEAD_SIZE * 4
    return pl.pallas_call(
        functools.partial(kernel, plan),
        out_shape=jax.ShapeDtypeStruct(out_shape, jnp.bfloat16),
        in_specs=[smem_spec()] + any_specs(8 + len(weights)) + [vmem_spec()] * 2,
        out_specs=vmem_spec(),
        scratch_shapes=[
            pltpu.VMEM((4 * rows, 2 * half), jnp.bfloat16),
            pltpu.VMEM((16 * depth, width), jnp.bfloat16),
            pltpu.SemaphoreType.DMA((24,)),
        ],
        compiler_params=pltpu.CompilerParams(vmem_limit_bytes=VMEM_LIMIT),
        cost_estimate=pl.CostEstimate(flops=flops, bytes_accessed=8 << 20, transcendentals=0),
    )(place, *tokens, *weights, cosine, sine)


def attend_kernel(place, queries, kv0, kv1, kv2, kv3, mine, other, store, sems):
    ctx, x = place[0], place[1]
    rows = kv0.shape[1]
    handles = []
    for r, ref in enumerate((kv0, kv1, kv2, kv3)):
        for m in range(4):
            block = ctx ^ (4 * m + r)
            into = store.at[pl.ds(pl.multiple_of(block * rows, rows), rows)]
            handles.append(pltpu.make_async_copy(ref.at[m], into, sems.at[4 * r + m]))
    for handle in handles:
        handle.start()
    for handle in handles:
        handle.wait()
    z, e = ctx // 4, ctx % 4
    scale = math.log2(math.e) / math.sqrt(HEAD_SIZE)
    span = 4 * rows
    heads = queries.shape[1] // rows
    group = 2
    row = lax.broadcasted_iota(jnp.int32, (group * rows, span), 0) % rows + e * rows
    column = lax.broadcasted_iota(jnp.int32, (group * rows, span), 1)
    allowed = column <= row

    def block_of(block, out):
        count = (block + 1) * span
        keys, values = store[:count, :HEAD_SIZE], store[:count, HEAD_SIZE:]
        for first in range(0, heads, group):
            query = queries[z ^ block, pl.ds(first * rows, group * rows), :]
            scores = lax.dot_general(
                query, keys, (((1,), (1,)), ((), ())), preferred_element_type=jnp.float32
            )
            last = jnp.where(allowed, scores[:, count - span :], jnp.float32(-1e30))
            scores = jnp.concatenate([scores[:, : count - span], last], axis=1) if block else last
            top = jnp.max(scores, axis=1, keepdims=True)
            weights = jnp.exp2((scores - top) * jnp.float32(scale))
            total = jnp.sum(weights, axis=1, keepdims=True)
            summed = jnp.dot(
                weights.astype(jnp.bfloat16), values, preferred_element_type=jnp.float32
            )
            normed = (summed / total).astype(jnp.bfloat16)
            for k in range(group):
                at = slice((first + k) * HEAD_SIZE, (first + k + 1) * HEAD_SIZE)
                out[block // 2, :, at] = normed[k * rows : (k + 1) * rows]

    @pl.when(x == 0)
    def _():
        for block in range(4):
            block_of(block, mine if block in (0, 3) else other)

    @pl.when(x == 1)
    def _():
        for block in range(4):
            block_of(block, mine if block in (1, 2) else other)


def attend(place, queries, kv):
    _, stacked, _ = queries.shape
    rows = kv[0].shape[1]
    heads = stacked // rows
    shape = jax.ShapeDtypeStruct((2, rows, heads * HEAD_SIZE), jnp.bfloat16)
    work = 4 * stacked * 16 * rows * HEAD_SIZE
    return pl.pallas_call(
        attend_kernel,
        out_shape=(shape, shape),
        in_specs=[smem_spec(), vmem_spec()] + any_specs(4),
        out_specs=(vmem_spec(), vmem_spec()),
        scratch_shapes=[
            pltpu.VMEM((16 * rows, 2 * HEAD_SIZE), jnp.bfloat16),
            pltpu.SemaphoreType.DMA((16,)),
        ],
        compiler_params=pltpu.CompilerParams(vmem_limit_bytes=VMEM_LIMIT),
        cost_estimate=pl.CostEstimate(
            flops=60 * work, bytes_accessed=4 << 20, transcendentals=4 * stacked * 16 * rows
        ),
    )(place, queries, *kv)


def output_kernel(place, *refs):
    attn_refs, weight_refs = refs[:8], refs[8:16]
    out0, out1, attn, wgt, sems = refs[16:]
    ctx, x = place[0], place[1]
    z, y, c = ctx // 4, ctx // 2 % 2, ctx % 2
    _, rows, width = attn_refs[0].shape
    depth, cols = weight_refs[0].shape
    handles = []
    for rx in range(2):
        for m in range(4):
            at = (x ^ rx) * depth + (z ^ m) * width
            into = attn.at[:, :, pl.ds(pl.multiple_of(at, width), width)]
            n = rx * 4 + m
            handles.append(pltpu.make_async_copy(attn_refs[n], into, sems.at[n]))
    for n in range(8):
        ry, rx, rc = n // 4, n // 2 % 2, n % 2
        at = ((y ^ ry) * 2 + (c ^ rc)) * cols
        into = wgt.at[
            pl.ds(pl.multiple_of((x ^ rx) * depth, depth), depth),
            pl.ds(pl.multiple_of(at, cols), cols),
        ]
        handles.append(pltpu.make_async_copy(weight_refs[n], into, sems.at[8 + n]))
    for handle in handles:
        handle.start()
    for handle in handles:
        handle.wait()
    low = z % 2
    for part in range(4):
        at = slice(part * cols, (part + 1) * cols)
        terms = []
        for f in range(2):
            term = jnp.dot(
                attn[:, :, f * depth : (f + 1) * depth].reshape(2 * rows, depth),
                wgt[f * depth : (f + 1) * depth, at],
                preferred_element_type=jnp.float32,
            )
            terms.append(term.astype(jnp.bfloat16).astype(jnp.float32))
        mixed = (terms[0] + terms[1]).astype(jnp.bfloat16)
        first, second = mixed[:rows], mixed[rows:]

        @pl.when(low == 0)
        def _():
            out0[:, at] = first
            out1[:, at] = second

        @pl.when(low == 1)
        def _():
            out0[:, at] = second
            out1[:, at] = first


def project_out(place, attn, weights):
    _, rows, width = attn[0].shape
    depth, cols = weights[0].shape
    shape = jax.ShapeDtypeStruct((rows, 4 * cols), jnp.bfloat16)
    return pl.pallas_call(
        output_kernel,
        out_shape=(shape, shape),
        in_specs=[smem_spec()] + any_specs(16),
        out_specs=(vmem_spec(), vmem_spec()),
        scratch_shapes=[
            pltpu.VMEM((2, rows, 2 * depth), jnp.bfloat16),
            pltpu.VMEM((2 * depth, 4 * cols), jnp.bfloat16),
            pltpu.SemaphoreType.DMA((16,)),
        ],
        compiler_params=pltpu.CompilerParams(vmem_limit_bytes=VMEM_LIMIT),
        cost_estimate=pl.CostEstimate(
            flops=2 * 2 * rows * 2 * depth * 4 * cols, bytes_accessed=12 << 20, transcendentals=0
        ),
    )(place, *attn, *weights)


ORDER = {
    "far": ("other0",),
    "tok3": ("tok2", "tok1", "own_y"),
    "near": ("y_out",),
    "query2": ("far",),
    "query3": ("far", "tok3", "other1"),
    "other3": ("other1",),
    "query1": ("far", "near", "other1", "other0"),
    "kv_rest_y": ("y_out", "xy_out", "other2", "tok3"),
    "query31_y": ("kv_rest_y",),
    "kv_core": ("other3",),
    "query_core": ("own_kv",),
    "mine1": ("core_w", "core_x", "core_y"),
    "mine2": ("core_w", "core_x", "core_y", "core_xy"),
    "from_x": ("core_x", "core_y", "core_xy"),
    "from_x1": ("mine1", "queries"),
    "core_y_kv": ("queries",),
    "from_x3": ("query_core",),
    "y_out": ("other0",),
}


class Transfers:
    def __init__(self):
        self.there = {}

    def __call__(self, name, array, target):
        earlier = [self.there[k] for k in ORDER.get(name, ())]
        if earlier:
            array = lax.optimization_barrier((array, *earlier))[0]
        self.there[name] = lax.ppermute(array, AXES, moves(target))
        return self.there[name]


def to_z(m):
    return lambda z, y, c, x: (z ^ m, y, c, x)


def to_y(z, y, c, x):
    return (z, 1 - y, c, x)


def to_core(z, y, c, x):
    return (z, y, 1 - c, x)


def to_x(z, y, c, x):
    return (z, y, c, 1 - x)


def split_body(tokens, w_query, key_matrix, value_matrix, w_out):
    ctx, x = lax.axis_index("ctx"), lax.axis_index("fsdp")
    place = jnp.stack([ctx, x]).astype(jnp.int32)
    z = ctx // 4
    rows = tokens.shape[0]
    group, wide = w_query.shape[1] // 4, 2 * HEAD_SIZE
    send = Transfers()

    def columns(weight, head, width):
        return lax.dynamic_slice_in_dim(weight, head * width, width, 1)

    def pair(head):
        parts = [columns(w, head, HEAD_SIZE) for w in (key_matrix, value_matrix)]
        return jnp.concatenate(parts, axis=1)

    tok1 = send("tok1", tokens, to_z(1))
    tok2 = send("tok2", tokens, to_z(2))
    other0 = send("other0", tokens, to_x)
    x_out = send("x_out", w_out, to_x)
    own = jnp.concatenate([pair(z), columns(w_query, z, group)], axis=1)
    own_y = send("own_y", own, to_y)
    y_out = send("y_out", w_out, to_y)
    far_half = [columns(w, 1 - z // 2, wide) for w in (key_matrix, value_matrix)]
    far = send("far", jnp.concatenate(far_half, axis=1), to_z(2))

    def far_pair(head):
        parts = [columns(w, head, HEAD_SIZE) for w in (far[:, :wide], far[:, wide:])]
        return jnp.concatenate(parts, axis=1)

    other1 = send("other1", tok1, to_x)
    tok3 = send("tok3", tok2, to_z(1))
    xy_out = send("xy_out", x_out, to_y)
    other2 = send("other2", tok2, to_x)
    near = send("near", jnp.stack([pair(z ^ 1), far_pair(1 - z % 2)]), to_z(1))
    query2 = send("query2", columns(w_query, z ^ 2, group), to_z(2))
    query3 = send("query3", columns(w_query, z ^ 3, group), to_z(3))
    other3 = send("other3", tok3, to_x)
    query1 = send("query1", columns(w_query, z ^ 1, group), to_z(1))
    token_pieces = [tokens, other0, tok1, other1, tok2, other2, tok3, other3]

    both = jnp.stack([own, own_y])
    both_core = send("both_core", both, to_core)
    kv_rest = jnp.stack([near[0], far_pair(z % 2), near[1]])
    kv_rest_y = send("kv_rest_y", kv_rest, to_y)
    query2_y = send("query2_y", query2, to_y)
    query31_y = send("query31_y", jnp.stack([query3, query1]), to_y)
    kv_core = send("kv_core", jnp.concatenate([kv_rest, kv_rest_y]), to_core)
    kv_weights = [both, both_core, kv_rest, kv_rest_y, kv_core]
    kv_plan = ((0, 2), (1, 3), (4, 8, 12), (6, 10, 14), (5, 9, 13, 7, 11, 15))

    slot = jnp.arange(4, dtype=jnp.int32)[:, None]
    positions = (ctx ^ (4 * slot)) * rows + jnp.arange(rows, dtype=jnp.int32)[None, :]
    cosine, sine = rotary_tables(positions.reshape(-1))
    cosine = jnp.concatenate([cosine, cosine], axis=1)
    sine = jnp.concatenate([-sine, sine], axis=1)

    own_kv = project(
        kv_kernel,
        (4, rows, wide),
        place,
        token_pieces,
        kv_weights,
        kv_plan,
        wide,
        cosine,
        sine,
    )
    send.there["own_kv"] = own_kv
    y_kv = send("y_kv", own_kv, to_y)
    core_kv = send("core_kv", own_kv, to_core)
    query_rest = jnp.stack([query1, query2, query3, query31_y[1], query2_y, query31_y[0]])
    query_core = send("query_core", query_rest, to_core)
    query_weights = [both, both_core, query_rest, query_core]
    query_plan = ((0, 2), (1, 3), (4, 8, 12, 6, 10, 14), (5, 9, 13, 7, 11, 15))
    queries = project(
        query_kernel,
        (4, group // HEAD_SIZE * rows, HEAD_SIZE),
        place,
        token_pieces,
        query_weights,
        query_plan,
        group,
        cosine,
        sine,
    )
    send.there["queries"] = queries
    core_y_kv = send("core_y_kv", y_kv, to_core)
    kv = [own_kv, core_kv, y_kv, core_y_kv]
    mine, other = attend(place, queries, kv)
    send.there["attend"] = mine
    out_weights = []
    for name, piece in (("w", w_out), ("x", x_out), ("y", y_out), ("xy", xy_out)):
        out_weights += [piece, send("core_" + name, piece, to_core)]
    mine2 = send("mine2", mine, to_z(2))
    mine1 = send("mine1", mine, to_z(1))
    from_x = send("from_x", other, to_x)
    from_x2 = send("from_x2", from_x, to_z(2))
    from_x1 = send("from_x1", from_x, to_z(1))
    mine3 = send("mine3", mine2, to_z(1))
    from_x3 = send("from_x3", from_x2, to_z(1))
    attn = [mine, mine1, mine2, mine3, from_x, from_x1, from_x2, from_x3]

    first, second = project_out(place, attn, out_weights)

    def home(m):
        return lambda z, y, c, x: (x ^ 3 * (z % 2 ^ m), y, c, z // 2)

    first, second = send("home0", first, home(0)), send("home1", second, home(1))
    odd = z // 2 == 1
    return jnp.concatenate(
        [jnp.where(odd, second, first), jnp.where(odd, first, second)], axis=1
    )


def solution(mesh):
    in_specs = (
        P("ctx", "fsdp"),
        P("ctx", "fsdp"),
        P("ctx", "fsdp"),
        P("ctx", "fsdp"),
        P("fsdp", "ctx"),
    )
    out_specs = P("ctx", "fsdp")
    split = mesh.shape["ctx"] == 16 and mesh.shape["fsdp"] == 2
    body = split_body if split else gathered_body
    return jax.shard_map(body, mesh=mesh, in_specs=in_specs, out_specs=out_specs, check_vma=False)
```

```python
import functools
import math

import jax
import jax.numpy as jnp
from jax import lax
from jax.experimental import pallas as pl
from jax.experimental.pallas import tpu as pltpu
from jax.sharding import PartitionSpec as P

HEAD_SIZE = 128
AXES = ("ctx", "fsdp")
VMEM_LIMIT = 18 * 1024 * 1024


def rotary_tables(positions):
    half_dim = HEAD_SIZE // 2
    inverse_freq = jnp.power(
        jnp.float32(500000.0), -jnp.arange(half_dim, dtype=jnp.float32) * 2.0 / HEAD_SIZE
    )
    angles = positions.astype(jnp.float32)[:, None] * inverse_freq[None, :]
    return jnp.cos(angles), jnp.sin(angles)


def rotate_heads(values, positions):
    tok_count = values.shape[0]
    head_count = values.shape[1] // HEAD_SIZE
    half_dim = HEAD_SIZE // 2
    cosine, sine_table = rotary_tables(positions)
    cosine, sine_table = cosine[:, None, :], sine_table[:, None, :]
    shaped = values.reshape(tok_count, head_count, HEAD_SIZE)
    first_half = shaped[:, :, :half_dim]
    second = shaped[:, :, half_dim:]
    turned = jnp.concatenate(
        [first_half * cosine - second * sine_table, second * cosine + first_half * sine_table],
        axis=2,
    )
    return turned.reshape(tok_count, head_count * HEAD_SIZE).astype(jnp.bfloat16)


def gathered_body(tokens, w_query, key_matrix, value_matrix, w_out):
    features = lax.all_gather(tokens, "fsdp", axis=1, tiled=True)
    tok_count = features.shape[0]
    positions = lax.axis_index("ctx") * tok_count + jnp.arange(tok_count, dtype=jnp.int32)

    def add_rows(weight_piece):
        return jnp.dot(features, weight_piece, preferred_element_type=jnp.float32)

    query_sum = add_rows(lax.all_gather(w_query, "ctx", axis=0, tiled=True))
    key_sum = add_rows(lax.all_gather(key_matrix, "ctx", axis=0, tiled=True))
    value_sum = add_rows(lax.all_gather(value_matrix, "ctx", axis=0, tiled=True))
    queries = rotate_heads(query_sum, positions)
    projected_keys = rotate_heads(key_sum, positions)
    projected_values = value_sum.astype(jnp.bfloat16)
    kv_heads = projected_keys.shape[1] // HEAD_SIZE
    queries_per_group = queries.shape[1] // projected_keys.shape[1]
    stacked = (
        queries.reshape(tok_count, kv_heads, queries_per_group, HEAD_SIZE)
        .transpose(1, 2, 0, 3)
        .reshape(kv_heads, queries_per_group * tok_count, HEAD_SIZE)
    )
    query_pos = jnp.tile(positions, queries_per_group)
    score_scale = 1.0 / math.sqrt(HEAD_SIZE)

    def update(attn_state, key_block, value_block, key_start):
        row_max, row_total, accum = attn_state
        block_rows = key_block.shape[0]
        key_heads = key_block.reshape(block_rows, kv_heads, HEAD_SIZE)
        value_heads = value_block.reshape(block_rows, kv_heads, HEAD_SIZE)
        scores = (
            jnp.einsum("gqd,kgd->gqk", stacked, key_heads, preferred_element_type=jnp.float32)
            * score_scale
        )
        key_pos = key_start + jnp.arange(block_rows, dtype=jnp.int32)
        allowed = (key_pos[None, :] <= query_pos[:, None])[None]
        masked = jnp.where(allowed, scores, jnp.float32(-1e30))
        new_max = jnp.maximum(row_max, jnp.max(masked, axis=2))
        exp_weights = jnp.where(allowed, jnp.exp(masked - new_max[:, :, None]), jnp.float32(0.0))
        factor = jnp.exp(row_max - new_max)
        row_total = row_total * factor + jnp.sum(exp_weights, axis=2)
        accum = accum * factor[:, :, None] + jnp.einsum(
            "gqk,kgd->gqd",
            exp_weights.astype(jnp.bfloat16),
            value_heads,
            preferred_element_type=jnp.float32,
        )
        return (new_max, row_total, accum)

    query_rows = queries_per_group * tok_count
    initial = (
        jnp.full((kv_heads, query_rows), -1e30, jnp.float32),
        jnp.zeros((kv_heads, query_rows), jnp.float32),
        jnp.zeros((kv_heads, query_rows, HEAD_SIZE), jnp.float32),
    )
    key_piece = lax.all_gather(projected_keys, "ctx", axis=0, tiled=True)
    value_piece = lax.all_gather(projected_values, "ctx", axis=0, tiled=True)
    block_rows = min(tok_count, key_piece.shape[0])
    block_count = key_piece.shape[0] // block_rows

    def advance(block_index, carried):
        key_start = block_index * block_rows
        key_block = lax.dynamic_slice_in_dim(key_piece, block_index * block_rows, block_rows, 0)
        value_block = lax.dynamic_slice_in_dim(value_piece, block_index * block_rows, block_rows, 0)
        return update(carried, key_block, value_block, key_start)

    row_max, row_total, accum = lax.fori_loop(0, block_count, advance, initial)
    normed = accum / row_total[:, :, None]
    attn_out = (
        normed.reshape(kv_heads, queries_per_group, tok_count, HEAD_SIZE)
        .transpose(2, 0, 1, 3)
        .reshape(tok_count, kv_heads * queries_per_group * HEAD_SIZE)
        .astype(jnp.bfloat16)
    )
    partial_out = jnp.dot(
        attn_out,
        lax.all_gather(w_out, "ctx", axis=1, tiled=True),
        preferred_element_type=jnp.float32,
    )
    return lax.psum_scatter(
        partial_out.astype(jnp.bfloat16), "fsdp", scatter_dimension=1, tiled=True
    )


def moves(target):
    pairs = []
    for i in range(32):
        z, y, c, x = i // 8, i // 4 % 2, i // 2 % 2, i % 2
        tz, ty, tc, tx = target(z, y, c, x)
        pairs.append((i, tz * 8 + ty * 4 + tc * 2 + tx))
    return pairs


def any_specs(count):
    return [pl.BlockSpec(memory_space=pl.ANY)] * count


def smem_spec():
    return pl.BlockSpec(memory_space=pltpu.SMEM)


def vmem_spec():
    return pl.BlockSpec(memory_space=pltpu.VMEM)


def load_projection(place, token_refs, weight_refs, plan, first_column, tok, wgt, sems):
    ctx, x = place[0], place[1]
    rows, half = token_refs[0].shape
    depth, width = wgt.shape[0] // 16, wgt.shape[1]
    copies = []
    for m in range(4):
        for rx in range(2):
            into = tok.at[pl.ds(m * rows, rows), pl.ds(pl.multiple_of((x ^ rx) * half, half), half)]
            copies.append((token_refs[m * 2 + rx], into))
    for ref, blocks in zip(weight_refs, plan, strict=True):
        at = first_column if ref.shape[-1] > width else 0
        for k, relative in enumerate(blocks):
            into = wgt.at[pl.ds(pl.multiple_of((ctx ^ relative) * depth, depth), depth)]
            copies.append((ref.at[k, :, pl.ds(at, width)], into))
    handles = [pltpu.make_async_copy(s, d, sems.at[i]) for i, (s, d) in enumerate(copies)]
    for handle in handles:
        handle.start()
    for handle in handles:
        handle.wait()


def rotated(values, cosine, sine):
    turned = jnp.concatenate([values[:, HEAD_SIZE // 2 :], values[:, : HEAD_SIZE // 2]], axis=1)
    return values * cosine + turned * sine


def kv_kernel(plan, place, *refs):
    token_refs, weight_refs = refs[:8], refs[8:-6]
    cosine, sine, out, tok, wgt, sems = refs[-6:]
    load_projection(place, token_refs, weight_refs, plan, 0, tok, wgt, sems)
    rows = tok.shape[0] // 4
    values = jnp.dot(tok[...], wgt[...], preferred_element_type=jnp.float32)
    keys = rotated(values[:, :HEAD_SIZE], cosine[...], sine[...]).astype(jnp.bfloat16)
    vals = values[:, HEAD_SIZE:].astype(jnp.bfloat16)
    for m in range(4):
        out[m, :, :HEAD_SIZE] = keys[m * rows : (m + 1) * rows]
        out[m, :, HEAD_SIZE:] = vals[m * rows : (m + 1) * rows]


def query_kernel(plan, place, *refs):
    token_refs, weight_refs = refs[:8], refs[8:-6]
    cosine, sine, out, tok, wgt, sems = refs[-6:]
    load_projection(place, token_refs, weight_refs, plan, 2 * HEAD_SIZE, tok, wgt, sems)
    rows = tok.shape[0] // 4
    heads = wgt.shape[1] // HEAD_SIZE
    for pair in range(heads // 2):
        values = jnp.dot(
            tok[...],
            wgt[:, pair * 2 * HEAD_SIZE : (pair + 1) * 2 * HEAD_SIZE],
            preferred_element_type=jnp.float32,
        )
        for k in range(2):
            one = rotated(values[:, k * HEAD_SIZE : (k + 1) * HEAD_SIZE], cosine[...], sine[...])
            one = one.astype(jnp.bfloat16)
            head = pair * 2 + k
            for m in range(4):
                out[m, head * rows : (head + 1) * rows, :] = one[m * rows : (m + 1) * rows]


def project(kernel, out_shape, place, tokens, weights, plan, width, cosine, sine):
    rows, half = tokens[0].shape
    depth = weights[0].shape[1]
    flops = 1 * 4 * rows * 16 * depth * HEAD_SIZE * 4
    return pl.pallas_call(
        functools.partial(kernel, plan),
        out_shape=jax.ShapeDtypeStruct(out_shape, jnp.bfloat16),
        in_specs=[smem_spec()] + any_specs(8 + len(weights)) + [vmem_spec()] * 2,
        out_specs=vmem_spec(),
        scratch_shapes=[
            pltpu.VMEM((4 * rows, 2 * half), jnp.bfloat16),
            pltpu.VMEM((16 * depth, width), jnp.bfloat16),
            pltpu.SemaphoreType.DMA((24,)),
        ],
        compiler_params=pltpu.CompilerParams(vmem_limit_bytes=VMEM_LIMIT),
        cost_estimate=pl.CostEstimate(flops=flops, bytes_accessed=8 << 20, transcendentals=0),
    )(place, *tokens, *weights, cosine, sine)


def attend_kernel(place, queries, kv0, kv1, kv2, kv3, mine, other, store, sems):
    ctx, x = place[0], place[1]
    rows = kv0.shape[1]
    handles = []
    for r, ref in enumerate((kv0, kv1, kv2, kv3)):
        for m in range(4):
            block = ctx ^ (4 * m + r)
            into = store.at[pl.ds(pl.multiple_of(block * rows, rows), rows)]
            handles.append(pltpu.make_async_copy(ref.at[m], into, sems.at[4 * r + m]))
    for handle in handles:
        handle.start()
    for handle in handles:
        handle.wait()
    z, e = ctx // 4, ctx % 4
    scale = math.log2(math.e) / math.sqrt(HEAD_SIZE)
    span = 4 * rows
    heads = queries.shape[1] // rows
    group = 2
    row = lax.broadcasted_iota(jnp.int32, (group * rows, span), 0) % rows + e * rows
    column = lax.broadcasted_iota(jnp.int32, (group * rows, span), 1)
    allowed = column <= row

    def block_of(block, out):
        count = (block + 1) * span
        keys, values = store[:count, :HEAD_SIZE], store[:count, HEAD_SIZE:]
        for first in range(0, heads, group):
            query = queries[z ^ block, pl.ds(first * rows, group * rows), :]
            scores = lax.dot_general(
                query, keys, (((1,), (1,)), ((), ())), preferred_element_type=jnp.float32
            )
            last = jnp.where(allowed, scores[:, count - span :], jnp.float32(-1e30))
            scores = jnp.concatenate([scores[:, : count - span], last], axis=1) if block else last
            top = jnp.max(scores, axis=1, keepdims=True)
            weights = jnp.exp2((scores - top) * jnp.float32(scale))
            total = jnp.sum(weights, axis=1, keepdims=True)
            summed = jnp.dot(
                weights.astype(jnp.bfloat16), values, preferred_element_type=jnp.float32
            )
            normed = (summed / total).astype(jnp.bfloat16)
            for k in range(group):
                at = slice((first + k) * HEAD_SIZE, (first + k + 1) * HEAD_SIZE)
                out[block // 2, :, at] = normed[k * rows : (k + 1) * rows]

    @pl.when(x == 0)
    def _():
        for block in range(4):
            block_of(block, mine if block in (0, 3) else other)

    @pl.when(x == 1)
    def _():
        for block in range(4):
            block_of(block, mine if block in (1, 2) else other)


def attend(place, queries, kv):
    _, stacked, _ = queries.shape
    rows = kv[0].shape[1]
    heads = stacked // rows
    shape = jax.ShapeDtypeStruct((2, rows, heads * HEAD_SIZE), jnp.bfloat16)
    work = 4 * stacked * 16 * rows * HEAD_SIZE
    return pl.pallas_call(
        attend_kernel,
        out_shape=(shape, shape),
        in_specs=[smem_spec(), vmem_spec()] + any_specs(4),
        out_specs=(vmem_spec(), vmem_spec()),
        scratch_shapes=[
            pltpu.VMEM((16 * rows, 2 * HEAD_SIZE), jnp.bfloat16),
            pltpu.SemaphoreType.DMA((16,)),
        ],
        compiler_params=pltpu.CompilerParams(vmem_limit_bytes=VMEM_LIMIT),
        cost_estimate=pl.CostEstimate(
            flops=60 * work, bytes_accessed=4 << 20, transcendentals=4 * stacked * 16 * rows
        ),
    )(place, queries, *kv)


def output_kernel(place, *refs):
    attn_refs, weight_refs = refs[:8], refs[8:16]
    out0, out1, attn, wgt, sems = refs[16:]
    ctx, x = place[0], place[1]
    z, y, c = ctx // 4, ctx // 2 % 2, ctx % 2
    _, rows, width = attn_refs[0].shape
    depth, cols = weight_refs[0].shape
    handles = []
    for rx in range(2):
        for m in range(4):
            at = (x ^ rx) * depth + (z ^ m) * width
            into = attn.at[:, :, pl.ds(pl.multiple_of(at, width), width)]
            n = rx * 4 + m
            handles.append(pltpu.make_async_copy(attn_refs[n], into, sems.at[n]))
    for n in range(8):
        ry, rx, rc = n // 4, n // 2 % 2, n % 2
        at = ((y ^ ry) * 2 + (c ^ rc)) * cols
        into = wgt.at[
            pl.ds(pl.multiple_of((x ^ rx) * depth, depth), depth),
            pl.ds(pl.multiple_of(at, cols), cols),
        ]
        handles.append(pltpu.make_async_copy(weight_refs[n], into, sems.at[8 + n]))
    for handle in handles:
        handle.start()
    for handle in handles:
        handle.wait()
    low = z % 2
    for part in range(4):
        at = slice(part * cols, (part + 1) * cols)
        terms = []
        for f in range(2):
            term = jnp.dot(
                attn[:, :, f * depth : (f + 1) * depth].reshape(2 * rows, depth),
                wgt[f * depth : (f + 1) * depth, at],
                preferred_element_type=jnp.float32,
            )
            terms.append(term.astype(jnp.bfloat16).astype(jnp.float32))
        mixed = (terms[0] + terms[1]).astype(jnp.bfloat16)
        first, second = mixed[:rows], mixed[rows:]

        @pl.when(low == 0)
        def _():
            out0[:, at] = first
            out1[:, at] = second

        @pl.when(low == 1)
        def _():
            out0[:, at] = second
            out1[:, at] = first


def project_out(place, attn, weights):
    _, rows, width = attn[0].shape
    depth, cols = weights[0].shape
    shape = jax.ShapeDtypeStruct((rows, 4 * cols), jnp.bfloat16)
    return pl.pallas_call(
        output_kernel,
        out_shape=(shape, shape),
        in_specs=[smem_spec()] + any_specs(16),
        out_specs=(vmem_spec(), vmem_spec()),
        scratch_shapes=[
            pltpu.VMEM((2, rows, 2 * depth), jnp.bfloat16),
            pltpu.VMEM((2 * depth, 4 * cols), jnp.bfloat16),
            pltpu.SemaphoreType.DMA((16,)),
        ],
        compiler_params=pltpu.CompilerParams(vmem_limit_bytes=VMEM_LIMIT),
        cost_estimate=pl.CostEstimate(
            flops=2 * 2 * rows * 2 * depth * 4 * cols, bytes_accessed=12 << 20, transcendentals=0
        ),
    )(place, *attn, *weights)


ORDER = {
    "far": ("other0",),
    "tok3": ("tok2", "tok1", "own_y"),
    "near": ("y_out",),
    "query2": ("far", "tok1"),
    "query3": ("far", "tok3", "other1"),
    "other3": ("other1",),
    "query1": ("far", "near", "other1", "other0"),
    "both_core": ("other1",),
    "kv_rest_y": ("y_out", "xy_out", "other2"),
    "query31_y": ("kv_rest_y",),
    "kv_core": ("other3",),
    "query_core": ("own_kv",),
    "mine1": ("core_w", "core_x", "core_y", "core_xy"),
    "mine2": ("core_w", "core_x", "core_y", "core_xy"),
    "from_x": ("core_x", "core_y", "core_xy"),
    "from_x1": ("mine1", "queries"),
    "core_y_kv": ("queries",),
    "from_x3": ("query_core",),
    "y_out": ("other0",),
}


class Transfers:
    def __init__(self):
        self.there = {}

    def __call__(self, name, array, target):
        earlier = [self.there[k] for k in ORDER.get(name, ())]
        if earlier:
            array = lax.optimization_barrier((array, *earlier))[0]
        self.there[name] = lax.ppermute(array, AXES, moves(target))
        return self.there[name]


def to_z(m):
    return lambda z, y, c, x: (z ^ m, y, c, x)


def to_y(z, y, c, x):
    return (z, 1 - y, c, x)


def to_core(z, y, c, x):
    return (z, y, 1 - c, x)


def to_x(z, y, c, x):
    return (z, y, c, 1 - x)


def split_body(tokens, w_query, key_matrix, value_matrix, w_out):
    ctx, x = lax.axis_index("ctx"), lax.axis_index("fsdp")
    place = jnp.stack([ctx, x]).astype(jnp.int32)
    z = ctx // 4
    rows = tokens.shape[0]
    group, wide = w_query.shape[1] // 4, 2 * HEAD_SIZE
    send = Transfers()

    def columns(weight, head, width):
        return lax.dynamic_slice_in_dim(weight, head * width, width, 1)

    def pair(head):
        parts = [columns(w, head, HEAD_SIZE) for w in (key_matrix, value_matrix)]
        return jnp.concatenate(parts, axis=1)

    tok1 = send("tok1", tokens, to_z(1))
    tok2 = send("tok2", tokens, to_z(2))
    other0 = send("other0", tokens, to_x)
    x_out = send("x_out", w_out, to_x)
    own = jnp.concatenate([pair(z), columns(w_query, z, group)], axis=1)
    own_y = send("own_y", own, to_y)
    y_out = send("y_out", w_out, to_y)
    far = send("far", jnp.stack([pair(z ^ 2), pair(z ^ 3)]), to_z(2))
    other1 = send("other1", tok1, to_x)
    tok3 = send("tok3", tok2, to_z(1))
    xy_out = send("xy_out", x_out, to_y)
    other2 = send("other2", tok2, to_x)
    near = send("near", jnp.stack([pair(z ^ 1), far[1]]), to_z(1))
    query2 = send("query2", columns(w_query, z ^ 2, group), to_z(2))
    query3 = send("query3", columns(w_query, z ^ 3, group), to_z(3))
    other3 = send("other3", tok3, to_x)
    query1 = send("query1", columns(w_query, z ^ 1, group), to_z(1))
    token_pieces = [tokens, other0, tok1, other1, tok2, other2, tok3, other3]

    both = jnp.stack([own, own_y])
    both_core = send("both_core", both, to_core)
    kv_rest = jnp.stack([near[0], far[0], near[1]])
    kv_rest_y = send("kv_rest_y", kv_rest, to_y)
    query2_y = send("query2_y", query2, to_y)
    query31_y = send("query31_y", jnp.stack([query3, query1]), to_y)
    kv_core = send("kv_core", jnp.concatenate([kv_rest, kv_rest_y]), to_core)
    kv_weights = [both, both_core, kv_rest, kv_rest_y, kv_core]
    kv_plan = ((0, 2), (1, 3), (4, 8, 12), (6, 10, 14), (5, 9, 13, 7, 11, 15))

    slot = jnp.arange(4, dtype=jnp.int32)[:, None]
    positions = (ctx ^ (4 * slot)) * rows + jnp.arange(rows, dtype=jnp.int32)[None, :]
    cosine, sine = rotary_tables(positions.reshape(-1))
    cosine = jnp.concatenate([cosine, cosine], axis=1)
    sine = jnp.concatenate([-sine, sine], axis=1)

    own_kv = project(
        kv_kernel,
        (4, rows, wide),
        place,
        token_pieces,
        kv_weights,
        kv_plan,
        wide,
        cosine,
        sine,
    )
    send.there["own_kv"] = own_kv
    y_kv = send("y_kv", own_kv, to_y)
    core_kv = send("core_kv", own_kv, to_core)
    query_rest = jnp.stack([query1, query2, query3, query31_y[1], query2_y, query31_y[0]])
    query_core = send("query_core", query_rest, to_core)
    query_weights = [both, both_core, query_rest, query_core]
    query_plan = ((0, 2), (1, 3), (4, 8, 12, 6, 10, 14), (5, 9, 13, 7, 11, 15))
    queries = project(
        query_kernel,
        (4, group // HEAD_SIZE * rows, HEAD_SIZE),
        place,
        token_pieces,
        query_weights,
        query_plan,
        group,
        cosine,
        sine,
    )
    send.there["queries"] = queries
    core_y_kv = send("core_y_kv", y_kv, to_core)
    kv = [own_kv, core_kv, y_kv, core_y_kv]
    mine, other = attend(place, queries, kv)
    send.there["attend"] = mine
    out_weights = []
    for name, piece in (("w", w_out), ("x", x_out), ("y", y_out), ("xy", xy_out)):
        out_weights += [piece, send("core_" + name, piece, to_core)]
    mine2 = send("mine2", mine, to_z(2))
    mine1 = send("mine1", mine, to_z(1))
    from_x = send("from_x", other, to_x)
    from_x2 = send("from_x2", from_x, to_z(2))
    from_x1 = send("from_x1", from_x, to_z(1))
    mine3 = send("mine3", mine2, to_z(1))
    from_x3 = send("from_x3", from_x2, to_z(1))
    attn = [mine, mine1, mine2, mine3, from_x, from_x1, from_x2, from_x3]

    first, second = project_out(place, attn, out_weights)

    def home(m):
        return lambda z, y, c, x: (x ^ 3 * (z % 2 ^ m), y, c, z // 2)

    first, second = send("home0", first, home(0)), send("home1", second, home(1))
    odd = z // 2 == 1
    return jnp.concatenate(
        [jnp.where(odd, second, first), jnp.where(odd, first, second)], axis=1
    )


def solution(mesh):
    in_specs = (
        P("ctx", "fsdp"),
        P("ctx", "fsdp"),
        P("ctx", "fsdp"),
        P("ctx", "fsdp"),
        P("fsdp", "ctx"),
    )
    out_specs = P("ctx", "fsdp")
    split = mesh.shape["ctx"] == 16 and mesh.shape["fsdp"] == 2
    body = split_body if split else gathered_body
    return jax.shard_map(body, mesh=mesh, in_specs=in_specs, out_specs=out_specs, check_vma=False)
```

```python
import functools
import math

import jax
import jax.numpy as jnp
from jax import lax
from jax.experimental import pallas as pl
from jax.experimental.pallas import tpu as pltpu
from jax.sharding import PartitionSpec as P

HEAD_SIZE = 128
AXES = ("ctx", "fsdp")
VMEM_LIMIT = 18 * 1024 * 1024


def rotary_tables(positions):
    half_dim = HEAD_SIZE // 2
    inverse_freq = jnp.power(
        jnp.float32(500000.0), -jnp.arange(half_dim, dtype=jnp.float32) * 2.0 / HEAD_SIZE
    )
    angles = positions.astype(jnp.float32)[:, None] * inverse_freq[None, :]
    return jnp.cos(angles), jnp.sin(angles)


def rotate_heads(values, positions):
    tok_count = values.shape[0]
    head_count = values.shape[1] // HEAD_SIZE
    half_dim = HEAD_SIZE // 2
    cosine, sine_table = rotary_tables(positions)
    cosine, sine_table = cosine[:, None, :], sine_table[:, None, :]
    shaped = values.reshape(tok_count, head_count, HEAD_SIZE)
    first_half = shaped[:, :, :half_dim]
    second = shaped[:, :, half_dim:]
    turned = jnp.concatenate(
        [first_half * cosine - second * sine_table, second * cosine + first_half * sine_table],
        axis=2,
    )
    return turned.reshape(tok_count, head_count * HEAD_SIZE).astype(jnp.bfloat16)


def gathered_body(tokens, w_query, key_matrix, value_matrix, w_out):
    features = lax.all_gather(tokens, "fsdp", axis=1, tiled=True)
    tok_count = features.shape[0]
    positions = lax.axis_index("ctx") * tok_count + jnp.arange(tok_count, dtype=jnp.int32)

    def add_rows(weight_piece):
        return jnp.dot(features, weight_piece, preferred_element_type=jnp.float32)

    query_sum = add_rows(lax.all_gather(w_query, "ctx", axis=0, tiled=True))
    key_sum = add_rows(lax.all_gather(key_matrix, "ctx", axis=0, tiled=True))
    value_sum = add_rows(lax.all_gather(value_matrix, "ctx", axis=0, tiled=True))
    queries = rotate_heads(query_sum, positions)
    projected_keys = rotate_heads(key_sum, positions)
    projected_values = value_sum.astype(jnp.bfloat16)
    kv_heads = projected_keys.shape[1] // HEAD_SIZE
    queries_per_group = queries.shape[1] // projected_keys.shape[1]
    stacked = (
        queries.reshape(tok_count, kv_heads, queries_per_group, HEAD_SIZE)
        .transpose(1, 2, 0, 3)
        .reshape(kv_heads, queries_per_group * tok_count, HEAD_SIZE)
    )
    query_pos = jnp.tile(positions, queries_per_group)
    score_scale = 1.0 / math.sqrt(HEAD_SIZE)

    def update(attn_state, key_block, value_block, key_start):
        row_max, row_total, accum = attn_state
        block_rows = key_block.shape[0]
        key_heads = key_block.reshape(block_rows, kv_heads, HEAD_SIZE)
        value_heads = value_block.reshape(block_rows, kv_heads, HEAD_SIZE)
        scores = (
            jnp.einsum("gqd,kgd->gqk", stacked, key_heads, preferred_element_type=jnp.float32)
            * score_scale
        )
        key_pos = key_start + jnp.arange(block_rows, dtype=jnp.int32)
        allowed = (key_pos[None, :] <= query_pos[:, None])[None]
        masked = jnp.where(allowed, scores, jnp.float32(-1e30))
        new_max = jnp.maximum(row_max, jnp.max(masked, axis=2))
        exp_weights = jnp.where(allowed, jnp.exp(masked - new_max[:, :, None]), jnp.float32(0.0))
        factor = jnp.exp(row_max - new_max)
        row_total = row_total * factor + jnp.sum(exp_weights, axis=2)
        accum = accum * factor[:, :, None] + jnp.einsum(
            "gqk,kgd->gqd",
            exp_weights.astype(jnp.bfloat16),
            value_heads,
            preferred_element_type=jnp.float32,
        )
        return (new_max, row_total, accum)

    query_rows = queries_per_group * tok_count
    initial = (
        jnp.full((kv_heads, query_rows), -1e30, jnp.float32),
        jnp.zeros((kv_heads, query_rows), jnp.float32),
        jnp.zeros((kv_heads, query_rows, HEAD_SIZE), jnp.float32),
    )
    key_piece = lax.all_gather(projected_keys, "ctx", axis=0, tiled=True)
    value_piece = lax.all_gather(projected_values, "ctx", axis=0, tiled=True)
    block_rows = min(tok_count, key_piece.shape[0])
    block_count = key_piece.shape[0] // block_rows

    def advance(block_index, carried):
        key_start = block_index * block_rows
        key_block = lax.dynamic_slice_in_dim(key_piece, block_index * block_rows, block_rows, 0)
        value_block = lax.dynamic_slice_in_dim(value_piece, block_index * block_rows, block_rows, 0)
        return update(carried, key_block, value_block, key_start)

    row_max, row_total, accum = lax.fori_loop(0, block_count, advance, initial)
    normed = accum / row_total[:, :, None]
    attn_out = (
        normed.reshape(kv_heads, queries_per_group, tok_count, HEAD_SIZE)
        .transpose(2, 0, 1, 3)
        .reshape(tok_count, kv_heads * queries_per_group * HEAD_SIZE)
        .astype(jnp.bfloat16)
    )
    partial_out = jnp.dot(
        attn_out,
        lax.all_gather(w_out, "ctx", axis=1, tiled=True),
        preferred_element_type=jnp.float32,
    )
    return lax.psum_scatter(
        partial_out.astype(jnp.bfloat16), "fsdp", scatter_dimension=1, tiled=True
    )


def moves(target):
    pairs = []
    for i in range(32):
        z, y, c, x = i // 8, i // 4 % 2, i // 2 % 2, i % 2
        tz, ty, tc, tx = target(z, y, c, x)
        pairs.append((i, tz * 8 + ty * 4 + tc * 2 + tx))
    return pairs


def any_specs(count):
    return [pl.BlockSpec(memory_space=pl.ANY)] * count


def smem_spec():
    return pl.BlockSpec(memory_space=pltpu.SMEM)


def vmem_spec():
    return pl.BlockSpec(memory_space=pltpu.VMEM)


def load_projection(place, token_refs, weight_refs, plan, first_column, tok, wgt, sems):
    ctx, x = place[0], place[1]
    rows, half = token_refs[0].shape
    depth, width = wgt.shape[0] // 16, wgt.shape[1]
    copies = []
    for m in range(4):
        for rx in range(2):
            into = tok.at[pl.ds(m * rows, rows), pl.ds(pl.multiple_of((x ^ rx) * half, half), half)]
            copies.append((token_refs[m * 2 + rx], into))
    for ref, blocks in zip(weight_refs, plan, strict=True):
        at = first_column if ref.shape[-1] > width else 0
        for k, relative in enumerate(blocks):
            into = wgt.at[pl.ds(pl.multiple_of((ctx ^ relative) * depth, depth), depth)]
            copies.append((ref.at[k, :, pl.ds(at, width)], into))
    handles = [pltpu.make_async_copy(s, d, sems.at[i]) for i, (s, d) in enumerate(copies)]
    for handle in handles:
        handle.start()
    for handle in handles:
        handle.wait()


def rotated(values, cosine, sine):
    turned = jnp.concatenate([values[:, HEAD_SIZE // 2 :], values[:, : HEAD_SIZE // 2]], axis=1)
    return values * cosine + turned * sine


def kv_kernel(plan, place, *refs):
    token_refs, weight_refs = refs[:8], refs[8:-6]
    cosine, sine, out, tok, wgt, sems = refs[-6:]
    load_projection(place, token_refs, weight_refs, plan, 0, tok, wgt, sems)
    rows = tok.shape[0] // 4
    values = jnp.dot(tok[...], wgt[...], preferred_element_type=jnp.float32)
    keys = rotated(values[:, :HEAD_SIZE], cosine[...], sine[...]).astype(jnp.bfloat16)
    vals = values[:, HEAD_SIZE:].astype(jnp.bfloat16)
    for m in range(4):
        out[m, :, :HEAD_SIZE] = keys[m * rows : (m + 1) * rows]
        out[m, :, HEAD_SIZE:] = vals[m * rows : (m + 1) * rows]


def query_kernel(plan, place, *refs):
    token_refs, weight_refs = refs[:8], refs[8:-6]
    cosine, sine, out, tok, wgt, sems = refs[-6:]
    load_projection(place, token_refs, weight_refs, plan, 2 * HEAD_SIZE, tok, wgt, sems)
    rows = tok.shape[0] // 4
    heads = wgt.shape[1] // HEAD_SIZE
    for pair in range(heads // 2):
        values = jnp.dot(
            tok[...],
            wgt[:, pair * 2 * HEAD_SIZE : (pair + 1) * 2 * HEAD_SIZE],
            preferred_element_type=jnp.float32,
        )
        for k in range(2):
            one = rotated(values[:, k * HEAD_SIZE : (k + 1) * HEAD_SIZE], cosine[...], sine[...])
            one = one.astype(jnp.bfloat16)
            head = pair * 2 + k
            for m in range(4):
                out[m, head * rows : (head + 1) * rows, :] = one[m * rows : (m + 1) * rows]


def project(kernel, out_shape, place, tokens, weights, plan, width, cosine, sine):
    rows, half = tokens[0].shape
    depth = weights[0].shape[1]
    flops = 1 * 4 * rows * 16 * depth * HEAD_SIZE * 4
    return pl.pallas_call(
        functools.partial(kernel, plan),
        out_shape=jax.ShapeDtypeStruct(out_shape, jnp.bfloat16),
        in_specs=[smem_spec()] + any_specs(8 + len(weights)) + [vmem_spec()] * 2,
        out_specs=vmem_spec(),
        scratch_shapes=[
            pltpu.VMEM((4 * rows, 2 * half), jnp.bfloat16),
            pltpu.VMEM((16 * depth, width), jnp.bfloat16),
            pltpu.SemaphoreType.DMA((24,)),
        ],
        compiler_params=pltpu.CompilerParams(vmem_limit_bytes=VMEM_LIMIT),
        cost_estimate=pl.CostEstimate(flops=flops, bytes_accessed=8 << 20, transcendentals=0),
    )(place, *tokens, *weights, cosine, sine)


def attend_kernel(place, queries, kv0, kv1, kv2, kv3, mine, other, store, sems):
    ctx, x = place[0], place[1]
    rows = kv0.shape[1]
    handles = []
    for r, ref in enumerate((kv0, kv1, kv2, kv3)):
        for m in range(4):
            block = ctx ^ (4 * m + r)
            into = store.at[pl.ds(pl.multiple_of(block * rows, rows), rows)]
            handles.append(pltpu.make_async_copy(ref.at[m], into, sems.at[4 * r + m]))
    for handle in handles:
        handle.start()
    for handle in handles:
        handle.wait()
    z, e = ctx // 4, ctx % 4
    scale = math.log2(math.e) / math.sqrt(HEAD_SIZE)
    span = 4 * rows
    heads = queries.shape[1] // rows
    group = 2
    row = lax.broadcasted_iota(jnp.int32, (group * rows, span), 0) % rows + e * rows
    column = lax.broadcasted_iota(jnp.int32, (group * rows, span), 1)
    allowed = column <= row

    def block_of(block, out):
        count = (block + 1) * span
        keys, values = store[:count, :HEAD_SIZE], store[:count, HEAD_SIZE:]
        for first in range(0, heads, group):
            query = queries[z ^ block, pl.ds(first * rows, group * rows), :]
            scores = lax.dot_general(
                query, keys, (((1,), (1,)), ((), ())), preferred_element_type=jnp.float32
            )
            last = jnp.where(allowed, scores[:, count - span :], jnp.float32(-1e30))
            scores = jnp.concatenate([scores[:, : count - span], last], axis=1) if block else last
            top = jnp.max(scores, axis=1, keepdims=True)
            weights = jnp.exp2((scores - top) * jnp.float32(scale))
            total = jnp.sum(weights, axis=1, keepdims=True)
            summed = jnp.dot(
                weights.astype(jnp.bfloat16), values, preferred_element_type=jnp.float32
            )
            normed = (summed / total).astype(jnp.bfloat16)
            for k in range(group):
                at = slice((first + k) * HEAD_SIZE, (first + k + 1) * HEAD_SIZE)
                out[block // 2, :, at] = normed[k * rows : (k + 1) * rows]

    @pl.when(x == 0)
    def _():
        for block in range(4):
            block_of(block, mine if block in (0, 3) else other)

    @pl.when(x == 1)
    def _():
        for block in range(4):
            block_of(block, mine if block in (1, 2) else other)


def attend(place, queries, kv):
    _, stacked, _ = queries.shape
    rows = kv[0].shape[1]
    heads = stacked // rows
    shape = jax.ShapeDtypeStruct((2, rows, heads * HEAD_SIZE), jnp.bfloat16)
    work = 4 * stacked * 16 * rows * HEAD_SIZE
    return pl.pallas_call(
        attend_kernel,
        out_shape=(shape, shape),
        in_specs=[smem_spec(), vmem_spec()] + any_specs(4),
        out_specs=(vmem_spec(), vmem_spec()),
        scratch_shapes=[
            pltpu.VMEM((16 * rows, 2 * HEAD_SIZE), jnp.bfloat16),
            pltpu.SemaphoreType.DMA((16,)),
        ],
        compiler_params=pltpu.CompilerParams(vmem_limit_bytes=VMEM_LIMIT),
        cost_estimate=pl.CostEstimate(
            flops=60 * work, bytes_accessed=4 << 20, transcendentals=4 * stacked * 16 * rows
        ),
    )(place, queries, *kv)


def output_kernel(place, *refs):
    attn_refs, weight_refs = refs[:8], refs[8:16]
    out0, out1, attn, wgt, sems = refs[16:]
    ctx, x = place[0], place[1]
    z, y, c = ctx // 4, ctx // 2 % 2, ctx % 2
    _, rows, width = attn_refs[0].shape
    depth, cols = weight_refs[0].shape
    handles = []
    for rx in range(2):
        for m in range(4):
            at = (x ^ rx) * depth + (z ^ m) * width
            into = attn.at[:, :, pl.ds(pl.multiple_of(at, width), width)]
            n = rx * 4 + m
            handles.append(pltpu.make_async_copy(attn_refs[n], into, sems.at[n]))
    for n in range(8):
        ry, rx, rc = n // 4, n // 2 % 2, n % 2
        at = ((y ^ ry) * 2 + (c ^ rc)) * cols
        into = wgt.at[
            pl.ds(pl.multiple_of((x ^ rx) * depth, depth), depth),
            pl.ds(pl.multiple_of(at, cols), cols),
        ]
        handles.append(pltpu.make_async_copy(weight_refs[n], into, sems.at[8 + n]))
    for handle in handles:
        handle.start()
    for handle in handles:
        handle.wait()
    low = z % 2
    terms = []
    for f in range(2):
        term = jnp.dot(
            attn[:, :, f * depth : (f + 1) * depth].reshape(2 * rows, depth),
            wgt[f * depth : (f + 1) * depth, :],
            preferred_element_type=jnp.float32,
        )
        terms.append(term.astype(jnp.bfloat16).astype(jnp.float32))
    mixed = (terms[0] + terms[1]).astype(jnp.bfloat16)
    first, second = mixed[:rows], mixed[rows:]

    @pl.when(low == 0)
    def _():
        out0[...] = first
        out1[...] = second

    @pl.when(low == 1)
    def _():
        out0[...] = second
        out1[...] = first


def project_out(place, attn, weights):
    _, rows, width = attn[0].shape
    depth, cols = weights[0].shape
    shape = jax.ShapeDtypeStruct((rows, 4 * cols), jnp.bfloat16)
    return pl.pallas_call(
        output_kernel,
        out_shape=(shape, shape),
        in_specs=[smem_spec()] + any_specs(16),
        out_specs=(vmem_spec(), vmem_spec()),
        scratch_shapes=[
            pltpu.VMEM((2, rows, 2 * depth), jnp.bfloat16),
            pltpu.VMEM((2 * depth, 4 * cols), jnp.bfloat16),
            pltpu.SemaphoreType.DMA((16,)),
        ],
        compiler_params=pltpu.CompilerParams(vmem_limit_bytes=VMEM_LIMIT),
        cost_estimate=pl.CostEstimate(
            flops=2 * 2 * rows * 2 * depth * 4 * cols, bytes_accessed=12 << 20, transcendentals=0
        ),
    )(place, *attn, *weights)


ORDER = {
    "far": ("other0",),
    "tok3": ("tok2", "tok1", "own_y"),
    "near": ("y_out",),
    "query2": ("far", "tok1"),
    "query3": ("far", "tok3", "other1"),
    "other3": ("other1",),
    "query1": ("far", "near", "other1", "other0"),
    "both_core": ("other1",),
    "kv_rest_y": ("y_out", "xy_out", "other2"),
    "query31_y": ("kv_rest_y",),
    "kv_core": ("other3",),
    "query_core": ("own_kv",),
    "mine1": ("core_w", "core_x", "core_y", "core_xy"),
    "mine2": ("core_w", "core_x", "core_y", "core_xy"),
    "from_x": ("core_x", "core_y", "core_xy"),
    "from_x1": ("mine1", "queries"),
    "core_y_kv": ("queries",),
    "from_x3": ("query_core",),
    "y_out": ("other0",),
}


class Transfers:
    def __init__(self):
        self.there = {}

    def __call__(self, name, array, target):
        earlier = [self.there[k] for k in ORDER.get(name, ())]
        if earlier:
            array = lax.optimization_barrier((array, *earlier))[0]
        self.there[name] = lax.ppermute(array, AXES, moves(target))
        return self.there[name]


def to_z(m):
    return lambda z, y, c, x: (z ^ m, y, c, x)


def to_y(z, y, c, x):
    return (z, 1 - y, c, x)


def to_core(z, y, c, x):
    return (z, y, 1 - c, x)


def to_x(z, y, c, x):
    return (z, y, c, 1 - x)


def split_body(tokens, w_query, key_matrix, value_matrix, w_out):
    ctx, x = lax.axis_index("ctx"), lax.axis_index("fsdp")
    place = jnp.stack([ctx, x]).astype(jnp.int32)
    z = ctx // 4
    rows = tokens.shape[0]
    group, wide = w_query.shape[1] // 4, 2 * HEAD_SIZE
    send = Transfers()

    def columns(weight, head, width):
        return lax.dynamic_slice_in_dim(weight, head * width, width, 1)

    def pair(head):
        parts = [columns(w, head, HEAD_SIZE) for w in (key_matrix, value_matrix)]
        return jnp.concatenate(parts, axis=1)

    tok1 = send("tok1", tokens, to_z(1))
    tok2 = send("tok2", tokens, to_z(2))
    other0 = send("other0", tokens, to_x)
    x_out = send("x_out", w_out, to_x)
    own = jnp.concatenate([pair(z), columns(w_query, z, group)], axis=1)
    own_y = send("own_y", own, to_y)
    y_out = send("y_out", w_out, to_y)
    far = send("far", jnp.stack([pair(z ^ 2), pair(z ^ 3)]), to_z(2))
    other1 = send("other1", tok1, to_x)
    tok3 = send("tok3", tok2, to_z(1))
    xy_out = send("xy_out", x_out, to_y)
    other2 = send("other2", tok2, to_x)
    near = send("near", jnp.stack([pair(z ^ 1), far[1]]), to_z(1))
    query2 = send("query2", columns(w_query, z ^ 2, group), to_z(2))
    query3 = send("query3", columns(w_query, z ^ 3, group), to_z(3))
    other3 = send("other3", tok3, to_x)
    query1 = send("query1", columns(w_query, z ^ 1, group), to_z(1))
    token_pieces = [tokens, other0, tok1, other1, tok2, other2, tok3, other3]

    both = jnp.stack([own, own_y])
    both_core = send("both_core", both, to_core)
    kv_rest = jnp.stack([near[0], far[0], near[1]])
    kv_rest_y = send("kv_rest_y", kv_rest, to_y)
    query2_y = send("query2_y", query2, to_y)
    query31_y = send("query31_y", jnp.stack([query3, query1]), to_y)
    kv_core = send("kv_core", jnp.concatenate([kv_rest, kv_rest_y]), to_core)
    kv_weights = [both, both_core, kv_rest, kv_rest_y, kv_core]
    kv_plan = ((0, 2), (1, 3), (4, 8, 12), (6, 10, 14), (5, 9, 13, 7, 11, 15))

    slot = jnp.arange(4, dtype=jnp.int32)[:, None]
    positions = (ctx ^ (4 * slot)) * rows + jnp.arange(rows, dtype=jnp.int32)[None, :]
    cosine, sine = rotary_tables(positions.reshape(-1))
    cosine = jnp.concatenate([cosine, cosine], axis=1)
    sine = jnp.concatenate([-sine, sine], axis=1)

    own_kv = project(
        kv_kernel,
        (4, rows, wide),
        place,
        token_pieces,
        kv_weights,
        kv_plan,
        wide,
        cosine,
        sine,
    )
    send.there["own_kv"] = own_kv
    y_kv = send("y_kv", own_kv, to_y)
    core_kv = send("core_kv", own_kv, to_core)
    query_rest = jnp.stack([query1, query2, query3, query31_y[1], query2_y, query31_y[0]])
    query_core = send("query_core", query_rest, to_core)
    query_weights = [both, both_core, query_rest, query_core]
    query_plan = ((0, 2), (1, 3), (4, 8, 12, 6, 10, 14), (5, 9, 13, 7, 11, 15))
    queries = project(
        query_kernel,
        (4, group // HEAD_SIZE * rows, HEAD_SIZE),
        place,
        token_pieces,
        query_weights,
        query_plan,
        group,
        cosine,
        sine,
    )
    send.there["queries"] = queries
    core_y_kv = send("core_y_kv", y_kv, to_core)
    kv = [own_kv, core_kv, y_kv, core_y_kv]
    mine, other = attend(place, queries, kv)
    send.there["attend"] = mine
    out_weights = []
    for name, piece in (("w", w_out), ("x", x_out), ("y", y_out), ("xy", xy_out)):
        out_weights += [piece, send("core_" + name, piece, to_core)]
    mine2 = send("mine2", mine, to_z(2))
    mine1 = send("mine1", mine, to_z(1))
    from_x = send("from_x", other, to_x)
    from_x2 = send("from_x2", from_x, to_z(2))
    from_x1 = send("from_x1", from_x, to_z(1))
    mine3 = send("mine3", mine2, to_z(1))
    from_x3 = send("from_x3", from_x2, to_z(1))
    attn = [mine, mine1, mine2, mine3, from_x, from_x1, from_x2, from_x3]

    first, second = project_out(place, attn, out_weights)

    def home(m):
        return lambda z, y, c, x: (x ^ 3 * (z % 2 ^ m), y, c, z // 2)

    first, second = send("home0", first, home(0)), send("home1", second, home(1))
    odd = z // 2 == 1
    return jnp.concatenate(
        [jnp.where(odd, second, first), jnp.where(odd, first, second)], axis=1
    )


def solution(mesh):
    in_specs = (
        P("ctx", "fsdp"),
        P("ctx", "fsdp"),
        P("ctx", "fsdp"),
        P("ctx", "fsdp"),
        P("fsdp", "ctx"),
    )
    out_specs = P("ctx", "fsdp")
    split = mesh.shape["ctx"] == 16 and mesh.shape["fsdp"] == 2
    body = split_body if split else gathered_body
    return jax.shard_map(body, mesh=mesh, in_specs=in_specs, out_specs=out_specs, check_vma=False)
```

```python
import functools
import math

import jax
import jax.numpy as jnp
from jax import lax
from jax.experimental import pallas as pl
from jax.experimental.pallas import tpu as pltpu
from jax.sharding import PartitionSpec as P

HEAD_SIZE = 128
AXES = ("ctx", "fsdp")
VMEM_LIMIT = 18 * 1024 * 1024


def rotary_tables(positions):
    half_dim = HEAD_SIZE // 2
    inverse_freq = jnp.power(
        jnp.float32(500000.0), -jnp.arange(half_dim, dtype=jnp.float32) * 2.0 / HEAD_SIZE
    )
    angles = positions.astype(jnp.float32)[:, None] * inverse_freq[None, :]
    return jnp.cos(angles), jnp.sin(angles)


def rotate_heads(values, positions):
    tok_count = values.shape[0]
    head_count = values.shape[1] // HEAD_SIZE
    half_dim = HEAD_SIZE // 2
    cosine, sine_table = rotary_tables(positions)
    cosine, sine_table = cosine[:, None, :], sine_table[:, None, :]
    shaped = values.reshape(tok_count, head_count, HEAD_SIZE)
    first_half = shaped[:, :, :half_dim]
    second = shaped[:, :, half_dim:]
    turned = jnp.concatenate(
        [first_half * cosine - second * sine_table, second * cosine + first_half * sine_table],
        axis=2,
    )
    return turned.reshape(tok_count, head_count * HEAD_SIZE).astype(jnp.bfloat16)


def gathered_body(tokens, w_query, key_matrix, value_matrix, w_out):
    features = lax.all_gather(tokens, "fsdp", axis=1, tiled=True)
    tok_count = features.shape[0]
    positions = lax.axis_index("ctx") * tok_count + jnp.arange(tok_count, dtype=jnp.int32)

    def add_rows(weight_piece):
        return jnp.dot(features, weight_piece, preferred_element_type=jnp.float32)

    query_sum = add_rows(lax.all_gather(w_query, "ctx", axis=0, tiled=True))
    key_sum = add_rows(lax.all_gather(key_matrix, "ctx", axis=0, tiled=True))
    value_sum = add_rows(lax.all_gather(value_matrix, "ctx", axis=0, tiled=True))
    queries = rotate_heads(query_sum, positions)
    projected_keys = rotate_heads(key_sum, positions)
    projected_values = value_sum.astype(jnp.bfloat16)
    kv_heads = projected_keys.shape[1] // HEAD_SIZE
    queries_per_group = queries.shape[1] // projected_keys.shape[1]
    stacked = (
        queries.reshape(tok_count, kv_heads, queries_per_group, HEAD_SIZE)
        .transpose(1, 2, 0, 3)
        .reshape(kv_heads, queries_per_group * tok_count, HEAD_SIZE)
    )
    query_pos = jnp.tile(positions, queries_per_group)
    score_scale = 1.0 / math.sqrt(HEAD_SIZE)

    def update(attn_state, key_block, value_block, key_start):
        row_max, row_total, accum = attn_state
        block_rows = key_block.shape[0]
        key_heads = key_block.reshape(block_rows, kv_heads, HEAD_SIZE)
        value_heads = value_block.reshape(block_rows, kv_heads, HEAD_SIZE)
        scores = (
            jnp.einsum("gqd,kgd->gqk", stacked, key_heads, preferred_element_type=jnp.float32)
            * score_scale
        )
        key_pos = key_start + jnp.arange(block_rows, dtype=jnp.int32)
        allowed = (key_pos[None, :] <= query_pos[:, None])[None]
        masked = jnp.where(allowed, scores, jnp.float32(-1e30))
        new_max = jnp.maximum(row_max, jnp.max(masked, axis=2))
        exp_weights = jnp.where(allowed, jnp.exp(masked - new_max[:, :, None]), jnp.float32(0.0))
        factor = jnp.exp(row_max - new_max)
        row_total = row_total * factor + jnp.sum(exp_weights, axis=2)
        accum = accum * factor[:, :, None] + jnp.einsum(
            "gqk,kgd->gqd",
            exp_weights.astype(jnp.bfloat16),
            value_heads,
            preferred_element_type=jnp.float32,
        )
        return (new_max, row_total, accum)

    query_rows = queries_per_group * tok_count
    initial = (
        jnp.full((kv_heads, query_rows), -1e30, jnp.float32),
        jnp.zeros((kv_heads, query_rows), jnp.float32),
        jnp.zeros((kv_heads, query_rows, HEAD_SIZE), jnp.float32),
    )
    key_piece = lax.all_gather(projected_keys, "ctx", axis=0, tiled=True)
    value_piece = lax.all_gather(projected_values, "ctx", axis=0, tiled=True)
    block_rows = min(tok_count, key_piece.shape[0])
    block_count = key_piece.shape[0] // block_rows

    def advance(block_index, carried):
        key_start = block_index * block_rows
        key_block = lax.dynamic_slice_in_dim(key_piece, block_index * block_rows, block_rows, 0)
        value_block = lax.dynamic_slice_in_dim(value_piece, block_index * block_rows, block_rows, 0)
        return update(carried, key_block, value_block, key_start)

    row_max, row_total, accum = lax.fori_loop(0, block_count, advance, initial)
    normed = accum / row_total[:, :, None]
    attn_out = (
        normed.reshape(kv_heads, queries_per_group, tok_count, HEAD_SIZE)
        .transpose(2, 0, 1, 3)
        .reshape(tok_count, kv_heads * queries_per_group * HEAD_SIZE)
        .astype(jnp.bfloat16)
    )
    partial_out = jnp.dot(
        attn_out,
        lax.all_gather(w_out, "ctx", axis=1, tiled=True),
        preferred_element_type=jnp.float32,
    )
    return lax.psum_scatter(
        partial_out.astype(jnp.bfloat16), "fsdp", scatter_dimension=1, tiled=True
    )


def moves(target):
    pairs = []
    for i in range(32):
        z, y, c, x = i // 8, i // 4 % 2, i // 2 % 2, i % 2
        tz, ty, tc, tx = target(z, y, c, x)
        pairs.append((i, tz * 8 + ty * 4 + tc * 2 + tx))
    return pairs


def any_specs(count):
    return [pl.BlockSpec(memory_space=pl.ANY)] * count


def smem_spec():
    return pl.BlockSpec(memory_space=pltpu.SMEM)


def vmem_spec():
    return pl.BlockSpec(memory_space=pltpu.VMEM)


def load_projection(place, token_refs, weight_refs, plan, first_column, tok, wgt, sems):
    ctx, x = place[0], place[1]
    rows, half = token_refs[0].shape
    depth, width = wgt.shape[0] // 16, wgt.shape[1]
    copies = []
    for m in range(4):
        for rx in range(2):
            into = tok.at[pl.ds(m * rows, rows), pl.ds(pl.multiple_of((x ^ rx) * half, half), half)]
            copies.append((token_refs[m * 2 + rx], into))
    for ref, blocks in zip(weight_refs, plan, strict=True):
        at = first_column if ref.shape[-1] > width else 0
        for k, relative in enumerate(blocks):
            into = wgt.at[pl.ds(pl.multiple_of((ctx ^ relative) * depth, depth), depth)]
            copies.append((ref.at[k, :, pl.ds(at, width)], into))
    handles = [pltpu.make_async_copy(s, d, sems.at[i]) for i, (s, d) in enumerate(copies)]
    for handle in handles:
        handle.start()
    for handle in handles:
        handle.wait()


def rotated(values, cosine, sine):
    turned = jnp.concatenate([values[:, HEAD_SIZE // 2 :], values[:, : HEAD_SIZE // 2]], axis=1)
    return values * cosine + turned * sine


def kv_kernel(plan, place, *refs):
    token_refs, weight_refs = refs[:8], refs[8:-6]
    cosine, sine, out, tok, wgt, sems = refs[-6:]
    load_projection(place, token_refs, weight_refs, plan, 0, tok, wgt, sems)
    rows = tok.shape[0] // 4
    values = jnp.dot(tok[...], wgt[...], preferred_element_type=jnp.float32)
    keys = rotated(values[:, :HEAD_SIZE], cosine[...], sine[...]).astype(jnp.bfloat16)
    vals = values[:, HEAD_SIZE:].astype(jnp.bfloat16)
    for m in range(4):
        out[m, :, :HEAD_SIZE] = keys[m * rows : (m + 1) * rows]
        out[m, :, HEAD_SIZE:] = vals[m * rows : (m + 1) * rows]


def query_kernel(plan, place, *refs):
    token_refs, weight_refs = refs[:8], refs[8:-6]
    cosine, sine, out, tok, wgt, sems = refs[-6:]
    load_projection(place, token_refs, weight_refs, plan, 2 * HEAD_SIZE, tok, wgt, sems)
    rows = tok.shape[0] // 4
    heads = wgt.shape[1] // HEAD_SIZE
    for pair in range(heads // 2):
        values = jnp.dot(
            tok[...],
            wgt[:, pair * 2 * HEAD_SIZE : (pair + 1) * 2 * HEAD_SIZE],
            preferred_element_type=jnp.float32,
        )
        for k in range(2):
            one = rotated(values[:, k * HEAD_SIZE : (k + 1) * HEAD_SIZE], cosine[...], sine[...])
            one = one.astype(jnp.bfloat16)
            head = pair * 2 + k
            for m in range(4):
                out[m, head * rows : (head + 1) * rows, :] = one[m * rows : (m + 1) * rows]


def project(kernel, out_shape, place, tokens, weights, plan, width, cosine, sine):
    rows, half = tokens[0].shape
    depth = weights[0].shape[1]
    flops = 1 * 4 * rows * 16 * depth * HEAD_SIZE * 4
    return pl.pallas_call(
        functools.partial(kernel, plan),
        out_shape=jax.ShapeDtypeStruct(out_shape, jnp.bfloat16),
        in_specs=[smem_spec()] + any_specs(8 + len(weights)) + [vmem_spec()] * 2,
        out_specs=vmem_spec(),
        scratch_shapes=[
            pltpu.VMEM((4 * rows, 2 * half), jnp.bfloat16),
            pltpu.VMEM((16 * depth, width), jnp.bfloat16),
            pltpu.SemaphoreType.DMA((24,)),
        ],
        compiler_params=pltpu.CompilerParams(vmem_limit_bytes=VMEM_LIMIT),
        cost_estimate=pl.CostEstimate(flops=flops, bytes_accessed=8 << 20, transcendentals=0),
    )(place, *tokens, *weights, cosine, sine)


def attend_kernel(place, queries, kv0, kv1, kv2, kv3, mine, other, store, sems):
    ctx, x = place[0], place[1]
    rows = kv0.shape[1]
    handles = []
    for r, ref in enumerate((kv0, kv1, kv2, kv3)):
        for m in range(4):
            block = ctx ^ (4 * m + r)
            into = store.at[pl.ds(pl.multiple_of(block * rows, rows), rows)]
            handles.append(pltpu.make_async_copy(ref.at[m], into, sems.at[4 * r + m]))
    for handle in handles:
        handle.start()
    for handle in handles:
        handle.wait()
    z, e = ctx // 4, ctx % 4
    scale = math.log2(math.e) / math.sqrt(HEAD_SIZE)
    span = 4 * rows
    heads = queries.shape[1] // rows
    group = 2
    row = lax.broadcasted_iota(jnp.int32, (group * rows, span), 0) % rows + e * rows
    column = lax.broadcasted_iota(jnp.int32, (group * rows, span), 1)
    allowed = column <= row

    def block_of(block, out):
        count = (block + 1) * span
        keys, values = store[:count, :HEAD_SIZE], store[:count, HEAD_SIZE:]
        for first in range(0, heads, group):
            query = queries[z ^ block, pl.ds(first * rows, group * rows), :]
            scores = lax.dot_general(
                query, keys, (((1,), (1,)), ((), ())), preferred_element_type=jnp.float32
            )
            last = jnp.where(allowed, scores[:, count - span :], jnp.float32(-1e30))
            scores = jnp.concatenate([scores[:, : count - span], last], axis=1) if block else last
            top = jnp.max(scores, axis=1, keepdims=True)
            weights = jnp.exp2((scores - top) * jnp.float32(scale))
            total = jnp.sum(weights, axis=1, keepdims=True)
            summed = jnp.dot(
                weights.astype(jnp.bfloat16), values, preferred_element_type=jnp.float32
            )
            normed = (summed / total).astype(jnp.bfloat16)
            for k in range(group):
                at = slice((first + k) * HEAD_SIZE, (first + k + 1) * HEAD_SIZE)
                out[block // 2, :, at] = normed[k * rows : (k + 1) * rows]

    @pl.when(x == 0)
    def _():
        for block in range(4):
            block_of(block, mine if block in (0, 3) else other)

    @pl.when(x == 1)
    def _():
        for block in range(4):
            block_of(block, mine if block in (1, 2) else other)


def attend(place, queries, kv):
    _, stacked, _ = queries.shape
    rows = kv[0].shape[1]
    heads = stacked // rows
    shape = jax.ShapeDtypeStruct((2, rows, heads * HEAD_SIZE), jnp.bfloat16)
    work = 4 * stacked * 16 * rows * HEAD_SIZE
    return pl.pallas_call(
        attend_kernel,
        out_shape=(shape, shape),
        in_specs=[smem_spec(), vmem_spec()] + any_specs(4),
        out_specs=(vmem_spec(), vmem_spec()),
        scratch_shapes=[
            pltpu.VMEM((16 * rows, 2 * HEAD_SIZE), jnp.bfloat16),
            pltpu.SemaphoreType.DMA((16,)),
        ],
        compiler_params=pltpu.CompilerParams(vmem_limit_bytes=VMEM_LIMIT),
        cost_estimate=pl.CostEstimate(
            flops=150 * work, bytes_accessed=4 << 20, transcendentals=4 * stacked * 16 * rows
        ),
    )(place, queries, *kv)


def output_kernel(place, *refs):
    attn_refs, weight_refs = refs[:8], refs[8:16]
    out0, out1, attn, wgt, sems = refs[16:]
    ctx, x = place[0], place[1]
    z, y, c = ctx // 4, ctx // 2 % 2, ctx % 2
    _, rows, width = attn_refs[0].shape
    depth, cols = weight_refs[0].shape
    handles = []
    for rx in range(2):
        for m in range(4):
            at = (x ^ rx) * depth + (z ^ m) * width
            into = attn.at[:, :, pl.ds(pl.multiple_of(at, width), width)]
            n = rx * 4 + m
            handles.append(pltpu.make_async_copy(attn_refs[n], into, sems.at[n]))
    for n in range(8):
        ry, rx, rc = n // 4, n // 2 % 2, n % 2
        at = ((y ^ ry) * 2 + (c ^ rc)) * cols
        into = wgt.at[
            pl.ds(pl.multiple_of((x ^ rx) * depth, depth), depth),
            pl.ds(pl.multiple_of(at, cols), cols),
        ]
        handles.append(pltpu.make_async_copy(weight_refs[n], into, sems.at[8 + n]))
    for handle in handles:
        handle.start()
    for handle in handles:
        handle.wait()
    low = z % 2
    terms = []
    for f in range(2):
        term = jnp.dot(
            attn[:, :, f * depth : (f + 1) * depth].reshape(2 * rows, depth),
            wgt[f * depth : (f + 1) * depth, :],
            preferred_element_type=jnp.float32,
        )
        terms.append(term.astype(jnp.bfloat16).astype(jnp.float32))
    mixed = (terms[0] + terms[1]).astype(jnp.bfloat16)
    first, second = mixed[:rows], mixed[rows:]

    @pl.when(low == 0)
    def _():
        out0[...] = first
        out1[...] = second

    @pl.when(low == 1)
    def _():
        out0[...] = second
        out1[...] = first


def project_out(place, attn, weights):
    _, rows, width = attn[0].shape
    depth, cols = weights[0].shape
    shape = jax.ShapeDtypeStruct((rows, 4 * cols), jnp.bfloat16)
    return pl.pallas_call(
        output_kernel,
        out_shape=(shape, shape),
        in_specs=[smem_spec()] + any_specs(16),
        out_specs=(vmem_spec(), vmem_spec()),
        scratch_shapes=[
            pltpu.VMEM((2, rows, 2 * depth), jnp.bfloat16),
            pltpu.VMEM((2 * depth, 4 * cols), jnp.bfloat16),
            pltpu.SemaphoreType.DMA((16,)),
        ],
        compiler_params=pltpu.CompilerParams(vmem_limit_bytes=VMEM_LIMIT),
        cost_estimate=pl.CostEstimate(
            flops=2 * 2 * rows * 2 * depth * 4 * cols, bytes_accessed=12 << 20, transcendentals=0
        ),
    )(place, *attn, *weights)


ORDER = {
    "far": ("other0",),
    "tok3": ("tok2", "tok1", "own_y"),
    "near": ("y_out",),
    "query2": ("far", "tok1"),
    "query3": ("far", "tok3", "other1"),
    "other3": ("other1",),
    "query1": ("far", "near", "other1", "other0"),
    "both_core": ("other1",),
    "kv_rest_y": ("y_out", "xy_out", "other2"),
    "query31_y": ("kv_rest_y",),
    "kv_core": ("other3",),
    "query_core": ("own_kv",),
    "mine1": ("core_w", "core_x", "core_y", "core_xy"),
    "mine2": ("core_w", "core_x", "core_y", "core_xy"),
    "from_x": ("core_x", "core_y", "core_xy"),
    "from_x1": ("mine1", "queries"),
    "core_y_kv": ("queries",),
    "from_x3": ("query_core",),
    "y_out": ("other0",),
}


class Transfers:
    def __init__(self):
        self.there = {}

    def __call__(self, name, array, target):
        earlier = [self.there[k] for k in ORDER.get(name, ())]
        if earlier:
            array = lax.optimization_barrier((array, *earlier))[0]
        self.there[name] = lax.ppermute(array, AXES, moves(target))
        return self.there[name]


def to_z(m):
    return lambda z, y, c, x: (z ^ m, y, c, x)


def to_y(z, y, c, x):
    return (z, 1 - y, c, x)


def to_core(z, y, c, x):
    return (z, y, 1 - c, x)


def to_x(z, y, c, x):
    return (z, y, c, 1 - x)


def split_body(tokens, w_query, key_matrix, value_matrix, w_out):
    ctx, x = lax.axis_index("ctx"), lax.axis_index("fsdp")
    place = jnp.stack([ctx, x]).astype(jnp.int32)
    z = ctx // 4
    rows = tokens.shape[0]
    group, wide = w_query.shape[1] // 4, 2 * HEAD_SIZE
    send = Transfers()

    def columns(weight, head, width):
        return lax.dynamic_slice_in_dim(weight, head * width, width, 1)

    def pair(head):
        parts = [columns(w, head, HEAD_SIZE) for w in (key_matrix, value_matrix)]
        return jnp.concatenate(parts, axis=1)

    tok1 = send("tok1", tokens, to_z(1))
    tok2 = send("tok2", tokens, to_z(2))
    other0 = send("other0", tokens, to_x)
    x_out = send("x_out", w_out, to_x)
    own = jnp.concatenate([pair(z), columns(w_query, z, group)], axis=1)
    own_y = send("own_y", own, to_y)
    y_out = send("y_out", w_out, to_y)
    far = send("far", jnp.stack([pair(z ^ 2), pair(z ^ 3)]), to_z(2))
    other1 = send("other1", tok1, to_x)
    tok3 = send("tok3", tok2, to_z(1))
    xy_out = send("xy_out", x_out, to_y)
    other2 = send("other2", tok2, to_x)
    near = send("near", jnp.stack([pair(z ^ 1), far[1]]), to_z(1))
    query2 = send("query2", columns(w_query, z ^ 2, group), to_z(2))
    query3 = send("query3", columns(w_query, z ^ 3, group), to_z(3))
    other3 = send("other3", tok3, to_x)
    query1 = send("query1", columns(w_query, z ^ 1, group), to_z(1))
    token_pieces = [tokens, other0, tok1, other1, tok2, other2, tok3, other3]

    both = jnp.stack([own, own_y])
    both_core = send("both_core", both, to_core)
    kv_rest = jnp.stack([near[0], far[0], near[1]])
    kv_rest_y = send("kv_rest_y", kv_rest, to_y)
    query2_y = send("query2_y", query2, to_y)
    query31_y = send("query31_y", jnp.stack([query3, query1]), to_y)
    kv_core = send("kv_core", jnp.concatenate([kv_rest, kv_rest_y]), to_core)
    kv_weights = [both, both_core, kv_rest, kv_rest_y, kv_core]
    kv_plan = ((0, 2), (1, 3), (4, 8, 12), (6, 10, 14), (5, 9, 13, 7, 11, 15))

    slot = jnp.arange(4, dtype=jnp.int32)[:, None]
    positions = (ctx ^ (4 * slot)) * rows + jnp.arange(rows, dtype=jnp.int32)[None, :]
    cosine, sine = rotary_tables(positions.reshape(-1))
    cosine = jnp.concatenate([cosine, cosine], axis=1)
    sine = jnp.concatenate([-sine, sine], axis=1)

    own_kv = project(
        kv_kernel,
        (4, rows, wide),
        place,
        token_pieces,
        kv_weights,
        kv_plan,
        wide,
        cosine,
        sine,
    )
    send.there["own_kv"] = own_kv
    y_kv = send("y_kv", own_kv, to_y)
    core_kv = send("core_kv", own_kv, to_core)
    query_rest = jnp.stack([query1, query2, query3, query31_y[1], query2_y, query31_y[0]])
    query_core = send("query_core", query_rest, to_core)
    query_weights = [both, both_core, query_rest, query_core]
    query_plan = ((0, 2), (1, 3), (4, 8, 12, 6, 10, 14), (5, 9, 13, 7, 11, 15))
    queries = project(
        query_kernel,
        (4, group // HEAD_SIZE * rows, HEAD_SIZE),
        place,
        token_pieces,
        query_weights,
        query_plan,
        group,
        cosine,
        sine,
    )
    send.there["queries"] = queries
    core_y_kv = send("core_y_kv", y_kv, to_core)
    kv = [own_kv, core_kv, y_kv, core_y_kv]
    mine, other = attend(place, queries, kv)
    send.there["attend"] = mine
    out_weights = []
    for name, piece in (("w", w_out), ("x", x_out), ("y", y_out), ("xy", xy_out)):
        out_weights += [piece, send("core_" + name, piece, to_core)]
    mine2 = send("mine2", mine, to_z(2))
    mine1 = send("mine1", mine, to_z(1))
    from_x = send("from_x", other, to_x)
    from_x2 = send("from_x2", from_x, to_z(2))
    from_x1 = send("from_x1", from_x, to_z(1))
    mine3 = send("mine3", mine2, to_z(1))
    from_x3 = send("from_x3", from_x2, to_z(1))
    attn = [mine, mine1, mine2, mine3, from_x, from_x1, from_x2, from_x3]

    first, second = project_out(place, attn, out_weights)

    def home(m):
        return lambda z, y, c, x: (x ^ 3 * (z % 2 ^ m), y, c, z // 2)

    first, second = send("home0", first, home(0)), send("home1", second, home(1))
    odd = z // 2 == 1
    return jnp.concatenate(
        [jnp.where(odd, second, first), jnp.where(odd, first, second)], axis=1
    )


def solution(mesh):
    in_specs = (
        P("ctx", "fsdp"),
        P("ctx", "fsdp"),
        P("ctx", "fsdp"),
        P("ctx", "fsdp"),
        P("fsdp", "ctx"),
    )
    out_specs = P("ctx", "fsdp")
    split = mesh.shape["ctx"] == 16 and mesh.shape["fsdp"] == 2
    body = split_body if split else gathered_body
    return jax.shard_map(body, mesh=mesh, in_specs=in_specs, out_specs=out_specs, check_vma=False)
```
